32 devices in a mesh: station: 32 (over z, y, x, core), sample: 1.
Axes of the slice: x: 2, y: 2, z: 4, core: 2. Of those that a mesh axis runs over, the one named last changes fastest.
Arguments:
- flux: bfloat16 [4, 1024, 3584], P('sample', 'station'), may hold values from -6 to 6
- coeff: float32 [1024, 3584], P('station'), may hold values from 0.02 to 0.24
- diff_steps: int32 [4], P('sample'), may hold values from 3 to 6, as said below
- footprint: bfloat16 [512, 4, 16384], P('station'), may hold values from -0.03125 to 0.03125
- tile_src: int32 [512, 4, 1], replicated, may hold values from 0 to 31; in each aligned block of 64 rows (0 to 63, 64 to 127, ..., all dimensions but the last counted through in order) at most 4 rows name the same one
- tile_local: int32 [512, 4], replicated, may hold values from 0 to 6
- tile_count: int32 [512], P('station'), may hold values from 1 to 4
Outputs:
- observed: float32 [512, 4], P('station')
The draws below stay inside these ranges and needn't reach their ends.
Inputs may be any that keep to these rules, and one draw needn't show every extreme that they name: `tile_src`: in each aligned block of 64 rows (the slots of one index's stations, stations and slots in order), no band appears more than 4 times, and some band appears exactly 4 times. `diff_steps`: some sample takes 6 steps and another takes 3.
All inputs are finite; a program needn't handle non-finite values.
Results may differ from the reference program's by a relative error of at most 0.0029.
Values may be sent and summed in bfloat16 or wider, within the bound.
A program may use at most 128 MiB of HBM per device.

```python
import math
import jax
import jax.numpy as jnp
import numpy as np
from jax import lax

STA_DEV = 16
ROWS_DEV = 32
TILE_LON = 512
TILES_DEV = 7
KT = 4
ITERS = 6
TILE = 16384
NLON = 3584
NLAT = 1024
SAMPLES = 4
STATIONS = 512
CAP = 4
N_STATION = 32


def draw_diff_steps(key, part):
    key_base = jax.random.fold_in(key, 11)
    key_first = jax.random.fold_in(key, 23)
    key_shift = jax.random.fold_in(key, 37)
    steps = jax.random.randint(key_base, (SAMPLES,), 3, ITERS + 1, dtype=jnp.int32)
    first = jax.random.randint(key_first, (), 0, SAMPLES, dtype=jnp.int32)
    shift = jax.random.randint(key_shift, (), 1, SAMPLES, dtype=jnp.int32)
    second = (first + shift) % SAMPLES
    positions = jnp.arange(SAMPLES, dtype=jnp.int32)
    steps = jnp.where(positions == first, ITERS, steps)
    steps = jnp.where(positions == second, 3, steps)
    return steps.astype(jnp.int32)


def with_ends(drawn, own_key, low, largest):
    extent = drawn.shape
    place = [jax.random.randint(jax.random.fold_in(own_key, axis), (), 0, extent[axis]) for axis in range(len(extent))]
    drawn = drawn.at[tuple(place)].set(low)
    longest = extent.index(max(extent))
    place[longest] = (place[longest] + 1) % extent[longest]
    return drawn.at[tuple(place)].set(largest)


def block_scale(key, extent, cuts, smallest, high):
    factor_of, own = 1.0, jax.random.fold_in(key, 6)
    for position, shards_of in cuts:
        steps = jnp.exp(jax.random.uniform(jax.random.fold_in(own, position), (shards_of,), jnp.float32, smallest / len(cuts), high / len(cuts)))
        factor_of = factor_of * jnp.repeat(steps, extent[position] // shards_of).reshape([-1 if axis == position else 1 for axis in range(len(extent))])
    return factor_of


def deal_out(own_key, own, number, rows, count, top, reach, skew):
    order = jax.random.permutation(own_key, count)
    packed, usual = shares(count, rows * top, reach, skew, True), shares(count, rows * top, reach, skew, False)
    places = jnp.arange(count)

    def named(tallies, turn):
        used = int((tallies > 0).sum())
        fixed = max(1, used // 4)
        moved = fixed + (places - fixed + turn * (used - fixed)) % max(1, count - fixed)
        return jnp.zeros((count,), jnp.int32).at[order[jnp.where(places < fixed, places, moved)]].set(jnp.asarray(tallies, jnp.int32))

    tallies = jnp.where(number % 4 == 0, named(packed, number // 4), named(usual, number - number // 4 - 1))
    mixed = jax.random.permutation(jax.random.fold_in(own, 3), count)
    giver, taker = mixed[0:count // 2 * 2:2], mixed[1:count // 2 * 2:2]
    room = jnp.minimum(tallies[giver] - 1, reach - tallies[taker]) // 2
    room = jnp.where((giver == order[0]) | (taker == order[0]) | (tallies[taker] == 0), 0, jnp.maximum(room, 0))
    moved = jax.random.randint(jax.random.fold_in(own, 4), (count // 2,), 0, 1 << 20) % (room + 1)
    tallies = tallies.at[giver].add(-moved).at[taker].add(moved)
    members = jnp.searchsorted(jnp.cumsum(tallies), jnp.arange(rows * top), side="right").astype(jnp.int32)
    grid = members.reshape(top, rows).T
    grid = grid[jax.random.permutation(jax.random.fold_in(own, 1), rows)]
    turn = jax.random.randint(jax.random.fold_in(own, 2), (rows, 1), 0, top)
    return jnp.take_along_axis(grid, (jnp.arange(top)[None, :] + turn) % top, axis=1)


def shares(number_of, total, most, lean, full):
    portions = [(1 << 20) // math.isqrt(rank ** lean) + 1 for rank in range(1, number_of + 1)]
    largest = most if full else min(most, max(-(-total // number_of), total * portions[0] // sum(portions)))
    least = 1 if total - largest >= number_of - 1 else 0
    given, surplus = [largest] + [least] * (number_of - 1), total - largest - least * (number_of - 1)
    while surplus > 0:
        movable = [i for i in range(1, number_of) if given[i] < largest] or [i for i in range(1, number_of) if given[i] < most]
        mass, budget = sum([portions[i] for i in movable]), surplus
        for i in movable:
            more = min(most - given[i], max(1, budget * portions[i] // mass), surplus)
            given[i] = given[i] + more
            surplus = surplus - more
    return np.array(given)


def scatter_about(stream_key, shape, scale, most, cuts=(), kind=jnp.bfloat16):
    result = scale * jax.random.normal(stream_key, shape, jnp.float32)
    if cuts:
        result = result * block_scale(stream_key, shape, cuts, -0.22, 0.18)
    return jnp.clip(result, -most, most).astype(kind)


def setup_inputs(seed: int = 0) -> dict:
    key_list = jax.random.split(jax.random.key(seed), 8)
    flux = scatter_about(key_list[0], (SAMPLES, NLAT, NLON), 1.0, 6.0, ((1, 32),))
    coeff = jnp.clip(jnp.exp(math.log(0.24) - 2.4849066 * jax.random.uniform(key_list[1], (NLAT, NLON), jnp.float32) ** block_scale(key_list[1], (NLAT, NLON), ((0, 32),), -0.2, 0.2)), 0.02, 0.24)
    diff_steps = draw_diff_steps(jax.random.fold_in(key_list[7], 71), 0)
    footprint = scatter_about(key_list[3], (STATIONS, KT, TILE), (TILE * 2) ** -0.5, 0.03125, ((0, 32),))
    tile_src_keys = jax.random.split(jax.random.fold_in(key_list[4], 1), STATIONS * KT // (STA_DEV * KT))
    tile_src_turns = jax.random.permutation(jax.random.fold_in(key_list[4], 3), STATIONS * KT // (STA_DEV * KT))
    tile_src = jax.vmap(lambda own, number: deal_out(jax.random.fold_in(key_list[4], 2), own, number, STA_DEV * KT, N_STATION, 1, CAP, 2))(tile_src_keys, tile_src_turns).reshape((STATIONS, KT, 1))
    tile_local = with_ends(jax.random.randint(key_list[5], (STATIONS, KT), 0, TILES_DEV), jax.random.fold_in(key_list[5], 1), 0, TILES_DEV - 1).astype(jnp.int32)
    tile_count = with_ends(jax.random.randint(key_list[6], (STATIONS,), 1, KT + 1), jax.random.fold_in(key_list[6], 1), 1, KT).astype(jnp.int32)
    return dict(flux=flux, coeff=coeff, diff_steps=diff_steps, footprint=footprint, tile_src=tile_src, tile_local=tile_local, tile_count=tile_count)


def reference(flux, coeff, diff_steps, footprint, tile_src, tile_local, tile_count):
    def diffuse_one(pair):
        sample_field, limit = pair
        field = sample_field.astype(jnp.float32)
        for step_index in range(ITERS):
            gate = (step_index < limit).astype(jnp.float32)
            padded = jnp.pad(field, ((1, 1), (0, 0)))
            lap = padded[:-2] + padded[2:] + jnp.roll(field, 1, 1) + jnp.roll(field, -1, 1) - 4.0 * field
            field = field + gate * coeff * lap
        return field.astype(jnp.bfloat16)

    final = lax.map(diffuse_one, (flux, diff_steps))
    tiles = final.reshape(SAMPLES, N_STATION, ROWS_DEV, TILES_DEV, TILE_LON)
    tiles = tiles.transpose(1, 3, 0, 2, 4).reshape(N_STATION * TILES_DEV, SAMPLES, TILE)

    def station_obs(group):
        prints, sources, locals_, count = group
        ids = (sources[:, 0] * TILES_DEV + locals_).astype(jnp.int32)
        picked = tiles[ids]
        values = jnp.einsum("kst,kt->ks", picked.astype(jnp.float32), prints.astype(jnp.float32))
        live = (jnp.arange(KT, dtype=jnp.int32) < count).astype(jnp.float32)
        return jnp.sum(values * live[:, None], axis=0)

    return lax.map(station_obs, (footprint, tile_src, tile_local, tile_count))
```

```python
import functools

import jax
import jax.numpy as jnp
from jax import lax
from jax.experimental import pallas as pl
from jax.experimental.pallas import tpu as pltpu
from jax.sharding import PartitionSpec as P

TILE_LON = 512
TILES_DEV = 7
LANES_T = 8
KT = 4
ITERS = 6
INNER = 8
CHUNKS = 4
MESH = pl.DeviceIdType.MESH


def east_west(x, lane, tile):
    width = x.shape[1]
    west = pltpu.roll(x, 1, 1)
    first = west[:, :128]
    before = jnp.where(tile == 0, pltpu.roll(first, 2, 0), pltpu.roll(first, 1, 0))
    first = jnp.where(lane == 0, before, first)
    west = jnp.concatenate([first, west[:, 128:]], axis=1)
    east = pltpu.roll(x, width - 1, 1)
    last = east[:, width - 128 :]
    after = jnp.where(tile == TILES_DEV - 1, pltpu.roll(last, 6, 0), pltpu.roll(last, 7, 0))
    last = jnp.where(lane == 127, after, last)
    east = jnp.concatenate([east[:, : width - 128], last], axis=1)
    return west, east


def kernel(
    outer_n, slots,
    gates, prints, hot, flux, coef, sel, group, weights,
    out,
    send, arr, halo_f, halo_c, field_a, field_b, cof, tiles, val, ret,
    f_send, f_recv, h_send, h_recv, r_send, r_recv, l_send, l_recv, v_send, v_recv,
):
    rows = flux.shape[0]
    wide = flux.shape[1]
    samples = wide // LANES_T
    count = outer_n * INNER
    me = lax.axis_index("station")
    outer, inner = me // INNER, lax.rem(me, INNER)
    base = outer * INNER
    has_up, has_down = me > 0, me < count - 1
    has_left, has_right = outer > 0, outer < outer_n - 1
    far_up = jnp.logical_and(has_up, inner == 0)
    far_down = jnp.logical_and(has_down, inner == INNER - 1)

    def peer(offset):
        return base + lax.rem(inner + offset, INNER)

    barrier = pltpu.get_barrier_semaphore()

    def greet(device):
        pl.semaphore_signal(barrier, inc=1, device_id={"station": device}, device_id_type=MESH)

    for offset in range(1, INNER):
        greet(peer(offset))
    others = ((has_left, -INNER), (has_right, INNER), (far_up, -1), (far_down, 1))
    for there, step in others:
        @pl.when(there)
        def _():
            greet(me + step)
    pl.semaphore_wait(barrier, INNER - 1 + sum(jnp.where(there, 1, 0) for there, _ in others))

    def remote(src, dst, ssem, rsem, device):
        return pltpu.make_async_remote_copy(
            src_ref=src, dst_ref=dst, send_sem=ssem, recv_sem=rsem,
            device_id={"station": device}, device_id_type=MESH,
        )

    def halo_copies(way):
        step = -1 if way == 0 else 1
        cut = pl.ds(0, ITERS) if way == 0 else pl.ds(rows - ITERS, ITERS)
        return (
            remote(flux.at[cut], halo_f.at[1 - way], h_send.at[way, 0], h_recv.at[1 - way, 0], me + step),
            remote(coef.at[cut], halo_c.at[1 - way], h_send.at[way, 1], h_recv.at[1 - way, 1], me + step),
        )

    for way, there in ((0, has_up), (1, has_down)):
        @pl.when(there)
        def _():
            for copy in halo_copies(way):
                copy.start()

        @pl.when(jnp.logical_not(there))
        def _():
            halo_f[way] = jnp.zeros(halo_f.shape[1:], halo_f.dtype)
            halo_c[way] = jnp.zeros(halo_c.shape[1:], halo_c.dtype)

    length = prints.shape[1] // CHUNKS

    def print_copy(offset, c):
        target = peer(offset)
        lanes = pl.ds(c * length, length)
        to_rows = pl.ds(pl.multiple_of(lax.rem(inner + offset, INNER) * slots, slots), slots)
        my_rows = pl.ds(pl.multiple_of(inner * slots, slots), slots)
        return remote(send.at[to_rows, lanes], arr.at[my_rows, lanes], f_send.at[offset, c], f_recv.at[offset, c], target)

    for c in range(CHUNKS):
        def pack(i, carry):
            lanes = pl.ds(pl.multiple_of(c * length + i * 512, 512), 512)
            send[:, lanes] = jnp.dot(hot[...], prints[:, lanes], preferred_element_type=jnp.float32).astype(jnp.bfloat16)
            return carry

        lax.fori_loop(0, length // 512, pack, 0)
        for offset in range(1, INNER):
            print_copy(offset, c).start()
    own = pl.ds(pl.multiple_of(inner * slots, slots), slots)
    arr[own, :] = send[own, :]

    def load(r, carry):
        field_a[r + ITERS] = flux[r].astype(jnp.float32)
        cof[r + ITERS] = coef[r]
        return carry

    lax.fori_loop(0, rows, load, 0)
    for way, there in ((0, has_up), (1, has_down)):
        @pl.when(there)
        def _():
            for copy in halo_copies(way):
                copy.wait_send()
            remote(flux.at[pl.ds(0, ITERS)], halo_f.at[way], h_send.at[way, 0], h_recv.at[way, 0], me).wait_recv()
            remote(coef.at[pl.ds(0, ITERS)], halo_c.at[way], h_send.at[way, 1], h_recv.at[way, 1], me).wait_recv()

    def load_halo(r, carry):
        field_a[r] = halo_f[0, r].astype(jnp.float32)
        cof[r] = halo_c[0, r]
        field_a[r + ITERS + rows] = halo_f[1, r].astype(jnp.float32)
        cof[r + ITERS + rows] = halo_c[1, r]
        return carry

    lax.fori_loop(0, ITERS, load_halo, 0)

    lane = lax.broadcasted_iota(jnp.int32, (LANES_T, 128), 1)
    tile = lax.broadcasted_iota(jnp.int32, (LANES_T, 128), 0)

    def updated(src, r, k, s):
        cut = slice(s * LANES_T, (s + 1) * LANES_T)
        center = src[r, cut, :]
        west, east = east_west(center, lane, tile)
        lap = src[r - 1, cut, :] + src[r + 1, cut, :] + west + east - 4.0 * center
        return center + gates[k, s] * cof[r] * lap

    src, dst = field_a, field_b
    for k in range(ITERS - 1):
        def one_row(r, carry, src=src, dst=dst, k=k):
            for s in range(samples):
                dst[r, s * LANES_T : (s + 1) * LANES_T, :] = updated(src, r, k, s)
            return carry

        lax.fori_loop(k + 1, rows + 2 * ITERS - 1 - k, one_row, 0)
        src, dst = dst, src

    piece = rows // CHUNKS

    def block_copy(block, c, k, to_right):
        at = tiles.at[pl.ds(c * piece, piece), pl.ds(pl.multiple_of(block * wide, wide), wide), :]
        if to_right:
            return remote(at, at, r_send.at[k, c], r_recv.at[k, c], me + INNER)
        return remote(at, at, l_send.at[k, c], l_recv.at[k, c], me - INNER)

    def start_block(block, c, k, to_right, there):
        @pl.when(jnp.logical_and(there, has_right if to_right else has_left))
        def _():
            block_copy(block, c, k, to_right).start()

    mine = pl.ds(pl.multiple_of(outer * wide, wide), wide)
    for c in range(CHUNKS):
        def last_row(r, carry, src=src):
            done = [updated(src, r + ITERS, ITERS - 1, s) for s in range(samples)]
            tiles[r, mine, :] = jnp.concatenate(done, axis=0).astype(jnp.bfloat16)
            return carry

        lax.fori_loop(c * piece, (c + 1) * piece, last_row, 0)
        start_block(outer, c, 0, True, has_right)
        start_block(outer, c, 0, False, has_left)

    acc = jnp.zeros((INNER * slots, outer_n * wide), jnp.float32)
    for k in range(outer_n - 1):
        for c in range(CHUNKS):
            from_left, from_right = outer - 1 - k >= 0, outer + 1 + k < outer_n

            @pl.when(from_left)
            def _():
                block_copy(outer - 1 - k, c, k, True).wait_recv()

            if k < outer_n - 2:
                start_block(outer - 1 - k, c, k + 1, True, from_left)

            @pl.when(from_right)
            def _():
                block_copy(outer + 1 + k, c, k, False).wait_recv()

            if k < outer_n - 2:
                start_block(outer + 1 + k, c, k + 1, False, from_right)

            if k == outer_n - 2:
                for offset in range(1, INNER):
                    print_copy(offset, c).wait_recv()

                def multiply(r, total):
                    lanes = pl.ds(pl.multiple_of(r * TILE_LON, TILE_LON), TILE_LON)
                    return total + lax.dot_general(
                        arr[:, lanes], tiles[r], (((1,), (1,)), ((), ())),
                        preferred_element_type=jnp.float32,
                    )

                acc = lax.fori_loop(c * piece, (c + 1) * piece, multiply, acc)

    val[...] = jnp.dot(acc * sel[...], group[...], precision=lax.Precision.HIGHEST, preferred_element_type=jnp.float32)

    def value_copy(offset):
        to_rows = pl.ds(pl.multiple_of(lax.rem(inner + offset, INNER) * slots, slots), slots)
        return remote(val.at[to_rows], ret.at[own], v_send.at[offset], v_recv.at[offset], peer(offset))

    for offset in range(1, INNER):
        value_copy(offset).start()
    ret[own, :] = val[own, :]
    for offset in range(1, INNER):
        value_copy(offset).wait_recv()
    out[...] = jnp.dot(weights[...], ret[...], precision=lax.Precision.HIGHEST, preferred_element_type=jnp.float32)

    for offset in range(1, INNER):
        value_copy(offset).wait_send()
        for c in range(CHUNKS):
            print_copy(offset, c).wait_send()
    for k in range(outer_n - 1):
        for c in range(CHUNKS):
            @pl.when(jnp.logical_and(outer - k >= 0, has_right))
            def _():
                block_copy(outer - k, c, k, True).wait_send()

            @pl.when(jnp.logical_and(outer + k < outer_n, has_left))
            def _():
                block_copy(outer + k, c, k, False).wait_send()


def body(flux, coeff, diff_steps, footprint, tile_src, tile_local, tile_count):
    samples, rows, _ = flux.shape
    stations = footprint.shape[0]
    devices = lax.axis_size("station")
    outer_n = devices // INNER
    me = lax.axis_index("station")
    outer, inner = me // INNER, me % INNER
    slot_count = stations * KT
    cap = 2 * max(1, (slot_count + devices - 1) // devices)
    slots = outer_n * cap
    wide = samples * LANES_T

    flux_t = flux.reshape(samples, rows, TILES_DEV, TILE_LON).transpose(1, 0, 2, 3)
    flux_t = jnp.pad(flux_t, ((0, 0), (0, 0), (0, 1), (0, 0))).reshape(rows, wide, TILE_LON)
    coef_t = jnp.pad(coeff.reshape(rows, TILES_DEV, TILE_LON), ((0, 0), (0, 1), (0, 0)))
    gates = (jnp.arange(ITERS, dtype=jnp.int32)[:, None] < diff_steps[None, :]).astype(jnp.float32)

    order = jnp.arange(slot_count, dtype=jnp.int32)
    src = lax.dynamic_slice_in_dim(tile_src.reshape(devices, slot_count), outer * INNER, INNER, 0)
    loc = lax.dynamic_slice_in_dim(tile_local.reshape(devices, slot_count), outer * INNER, INNER, 0)
    target = src % INNER
    same = (target[:, :, None] == target[:, None, :]) & (order[None, :] < order[:, None])[None]
    rank = jnp.sum(same.astype(jnp.int32), axis=2)
    places = jnp.arange(slots, dtype=jnp.int32)
    my_target = lax.dynamic_index_in_dim(target, inner, 0, keepdims=False)
    my_rank = lax.dynamic_index_in_dim(rank, inner, 0, keepdims=False)
    place = my_target * slots + my_rank
    hot = place[None, :] == jnp.arange(INNER * slots, dtype=jnp.int32)[:, None]
    chosen = (target[:, None, :] == inner) & (rank[:, None, :] == places[None, :, None])
    code = (src // INNER) * LANES_T + loc + 1
    named = jnp.sum(jnp.where(chosen, code[:, None, :], 0), axis=2).reshape(INNER * slots) - 1
    columns = jnp.arange(outer_n * wide, dtype=jnp.int32)
    column_code = (columns // wide) * LANES_T + columns % LANES_T
    sel = (named[:, None] == column_code[None, :]).astype(jnp.float32)
    group = ((columns % wide) // LANES_T)[:, None] == jnp.arange(128, dtype=jnp.int32)[None, :]
    live = order % KT < tile_count[order // KT]
    mine = (order // KT)[None, :] == jnp.arange(stations, dtype=jnp.int32)[:, None]
    hits = (mine & live[None, :])[:, :, None] & (place[None, :, None] == jnp.arange(INNER * slots, dtype=jnp.int32)[None, None, :])
    weights = jnp.sum(hits.astype(jnp.float32), axis=1)

    ext = rows + 2 * ITERS
    vmem = pl.BlockSpec(memory_space=pltpu.VMEM)
    dma = pltpu.SemaphoreType.DMA
    observed = pl.pallas_call(
        functools.partial(kernel, outer_n, slots),
        out_shape=jax.ShapeDtypeStruct((stations, 128), jnp.float32),
        in_specs=[pl.BlockSpec(memory_space=pltpu.SMEM)] + [vmem] * 7,
        out_specs=vmem,
        scratch_shapes=[
            pltpu.VMEM((INNER * slots, footprint.shape[2]), jnp.bfloat16),
            pltpu.VMEM((INNER * slots, footprint.shape[2]), jnp.bfloat16),
            pltpu.VMEM((2, ITERS, wide, TILE_LON), jnp.bfloat16),
            pltpu.VMEM((2, ITERS, LANES_T, TILE_LON), jnp.float32),
            pltpu.VMEM((ext, wide, TILE_LON), jnp.float32),
            pltpu.VMEM((ext, wide, TILE_LON), jnp.float32),
            pltpu.VMEM((ext, LANES_T, TILE_LON), jnp.float32),
            pltpu.VMEM((rows, outer_n * wide, TILE_LON), jnp.bfloat16),
            pltpu.VMEM((INNER * slots, 128), jnp.float32),
            pltpu.VMEM((INNER * slots, 128), jnp.float32),
            dma((INNER, CHUNKS)), dma((INNER, CHUNKS)),
            dma((2, 2)), dma((2, 2)),
            dma((outer_n - 1, CHUNKS)), dma((outer_n - 1, CHUNKS)),
            dma((outer_n - 1, CHUNKS)), dma((outer_n - 1, CHUNKS)),
            dma((INNER,)), dma((INNER,)),
        ],
        compiler_params=pltpu.CompilerParams(
            collective_id=0, has_side_effects=True, vmem_limit_bytes=48 * 1024 * 1024
        ),
    )(
        gates, footprint.reshape(slot_count, footprint.shape[2]), hot.astype(jnp.bfloat16),
        flux_t, coef_t, sel, group.astype(jnp.float32), weights,
    )
    return lax.all_gather(observed[:, :samples], "sample", axis=1, tiled=True)


def solution(mesh):
    in_specs = (
        P("sample", "station", None),
        P("station", None),
        P("sample"),
        P("station", None, None),
        P(),
        P(),
        P("station"),
    )
    out_specs = P("station", None)
    return jax.shard_map(body, mesh=mesh, in_specs=in_specs, out_specs=out_specs, check_vma=False)
```

```python
import functools

import jax
import jax.numpy as jnp
from jax import lax
from jax.experimental import pallas as pl
from jax.experimental.pallas import tpu as pltpu
from jax.sharding import PartitionSpec as P

TILE_LON = 512
TILES_DEV = 7
LANES_T = 8
KT = 4
ITERS = 6
INNER = 8
CHUNKS = 4
MESH = pl.DeviceIdType.MESH


def east_west(x, lane, tile):
    width = x.shape[1]
    west = pltpu.roll(x, 1, 1)
    first = west[:, :128]
    before = jnp.where(tile == 0, pltpu.roll(first, 2, 0), pltpu.roll(first, 1, 0))
    first = jnp.where(lane == 0, before, first)
    west = jnp.concatenate([first, west[:, 128:]], axis=1)
    east = pltpu.roll(x, width - 1, 1)
    last = east[:, width - 128 :]
    after = jnp.where(tile == TILES_DEV - 1, pltpu.roll(last, 6, 0), pltpu.roll(last, 7, 0))
    last = jnp.where(lane == 127, after, last)
    east = jnp.concatenate([east[:, : width - 128], last], axis=1)
    return west, east


def kernel(
    outer_n, slots,
    gates, prints, hot, flux, coef, sel, group, weights,
    out,
    send, arr, halo_f, halo_c, field_a, field_b, cof, tiles, val, ret,
    f_send, f_recv, h_send, h_recv, r_send, r_recv, l_send, l_recv, v_send, v_recv,
):
    rows = flux.shape[0]
    wide = flux.shape[1]
    samples = wide // LANES_T
    count = outer_n * INNER
    me = lax.axis_index("station")
    outer, inner = me // INNER, lax.rem(me, INNER)
    base = outer * INNER
    has_up, has_down = me > 0, me < count - 1
    has_left, has_right = outer > 0, outer < outer_n - 1
    far_up = jnp.logical_and(has_up, inner == 0)
    far_down = jnp.logical_and(has_down, inner == INNER - 1)

    def peer(offset):
        return base + lax.rem(inner + offset, INNER)

    barrier = pltpu.get_barrier_semaphore()

    def greet(device):
        pl.semaphore_signal(barrier, inc=1, device_id={"station": device}, device_id_type=MESH)

    for offset in range(1, INNER):
        greet(peer(offset))
    others = ((has_left, -INNER), (has_right, INNER), (far_up, -1), (far_down, 1))
    for there, step in others:
        @pl.when(there)
        def _():
            greet(me + step)
    pl.semaphore_wait(barrier, INNER - 1 + sum(jnp.where(there, 1, 0) for there, _ in others))

    def remote(src, dst, ssem, rsem, device):
        return pltpu.make_async_remote_copy(
            src_ref=src, dst_ref=dst, send_sem=ssem, recv_sem=rsem,
            device_id={"station": device}, device_id_type=MESH,
        )

    def halo_copies(way):
        step = -1 if way == 0 else 1
        cut = pl.ds(0, ITERS) if way == 0 else pl.ds(rows - ITERS, ITERS)
        return (
            remote(flux.at[cut], halo_f.at[1 - way], h_send.at[way, 0], h_recv.at[1 - way, 0], me + step),
            remote(coef.at[cut], halo_c.at[1 - way], h_send.at[way, 1], h_recv.at[1 - way, 1], me + step),
        )

    for way, there in ((0, has_up), (1, has_down)):
        @pl.when(there)
        def _():
            for copy in halo_copies(way):
                copy.start()

        @pl.when(jnp.logical_not(there))
        def _():
            halo_f[way] = jnp.zeros(halo_f.shape[1:], halo_f.dtype)
            halo_c[way] = jnp.zeros(halo_c.shape[1:], halo_c.dtype)

    length = prints.shape[1] // CHUNKS

    def print_copy(offset, c):
        target = peer(offset)
        lanes = pl.ds(c * length, length)
        to_rows = pl.ds(pl.multiple_of(lax.rem(inner + offset, INNER) * slots, slots), slots)
        my_rows = pl.ds(pl.multiple_of(inner * slots, slots), slots)
        return remote(send.at[to_rows, lanes], arr.at[my_rows, lanes], f_send.at[offset, c], f_recv.at[offset, c], target)

    for c in range(CHUNKS):
        def pack(i, carry):
            for j in range(4):
                lanes = pl.ds(pl.multiple_of(c * length + i * 1024 + j * 256, 256), 256)
                send[:, lanes] = jnp.dot(hot[...], prints[:, lanes], preferred_element_type=jnp.float32).astype(jnp.bfloat16)
            return carry

        lax.fori_loop(0, length // 1024, pack, 0)
        for offset in range(1, INNER):
            print_copy(offset, c).start()
    own = pl.ds(pl.multiple_of(inner * slots, slots), slots)
    arr[own, :] = send[own, :]

    def load(r, carry):
        field_a[r + ITERS] = flux[r].astype(jnp.float32)
        cof[r + ITERS] = coef[r]
        return carry

    lax.fori_loop(0, rows, load, 0)
    for way, there in ((0, has_up), (1, has_down)):
        @pl.when(there)
        def _():
            for copy in halo_copies(way):
                copy.wait_send()
            remote(flux.at[pl.ds(0, ITERS)], halo_f.at[way], h_send.at[way, 0], h_recv.at[way, 0], me).wait_recv()
            remote(coef.at[pl.ds(0, ITERS)], halo_c.at[way], h_send.at[way, 1], h_recv.at[way, 1], me).wait_recv()

    def load_halo(r, carry):
        field_a[r] = halo_f[0, r].astype(jnp.float32)
        cof[r] = halo_c[0, r]
        field_a[r + ITERS + rows] = halo_f[1, r].astype(jnp.float32)
        cof[r + ITERS + rows] = halo_c[1, r]
        return carry

    lax.fori_loop(0, ITERS, load_halo, 0)

    lane = lax.broadcasted_iota(jnp.int32, (LANES_T, 128), 1)
    tile = lax.broadcasted_iota(jnp.int32, (LANES_T, 128), 0)

    def updated(src, r, k, s):
        cut = slice(s * LANES_T, (s + 1) * LANES_T)
        center = src[r, cut, :]
        west, east = east_west(center, lane, tile)
        lap = src[r - 1, cut, :] + src[r + 1, cut, :] + west + east - 4.0 * center
        return center + gates[k, s] * cof[r] * lap

    src, dst = field_a, field_b
    for k in range(ITERS - 1):
        def row_pair(i, carry, src=src, dst=dst, k=k):
            for r in (k + 1 + 2 * i, k + 2 + 2 * i):
                for s in range(samples):
                    dst[r, s * LANES_T : (s + 1) * LANES_T, :] = updated(src, r, k, s)
            return carry

        lax.fori_loop(0, rows // 2 + ITERS - 1 - k, row_pair, 0)
        src, dst = dst, src

    piece = rows // CHUNKS

    def block_copy(block, c, k, to_right):
        at = tiles.at[pl.ds(c * piece, piece), pl.ds(pl.multiple_of(block * wide, wide), wide), :]
        if to_right:
            return remote(at, at, r_send.at[k, c], r_recv.at[k, c], me + INNER)
        return remote(at, at, l_send.at[k, c], l_recv.at[k, c], me - INNER)

    def start_block(block, c, k, to_right, there):
        @pl.when(jnp.logical_and(there, has_right if to_right else has_left))
        def _():
            block_copy(block, c, k, to_right).start()

    mine = pl.ds(pl.multiple_of(outer * wide, wide), wide)
    for c in range(CHUNKS):
        def last_pair(i, carry, src=src):
            for r in (c * piece + 2 * i, c * piece + 2 * i + 1):
                done = [updated(src, r + ITERS, ITERS - 1, s) for s in range(samples)]
                tiles[r, mine, :] = jnp.concatenate(done, axis=0).astype(jnp.bfloat16)
            return carry

        lax.fori_loop(0, piece // 2, last_pair, 0)
        start_block(outer, c, 0, True, has_right)
        start_block(outer, c, 0, False, has_left)

    acc = jnp.zeros((INNER * slots, outer_n * wide), jnp.float32)
    for k in range(outer_n - 1):
        for c in range(CHUNKS):
            from_left, from_right = outer - 1 - k >= 0, outer + 1 + k < outer_n

            @pl.when(from_left)
            def _():
                block_copy(outer - 1 - k, c, k, True).wait_recv()

            if k < outer_n - 2:
                start_block(outer - 1 - k, c, k + 1, True, from_left)

            @pl.when(from_right)
            def _():
                block_copy(outer + 1 + k, c, k, False).wait_recv()

            if k < outer_n - 2:
                start_block(outer + 1 + k, c, k + 1, False, from_right)

            if k == outer_n - 2:
                for offset in range(1, INNER):
                    print_copy(offset, c).wait_recv()

                def multiply(i, total):
                    for r in (c * piece + 2 * i, c * piece + 2 * i + 1):
                        lanes = pl.ds(pl.multiple_of(r * TILE_LON, TILE_LON), TILE_LON)
                        total = total + lax.dot_general(
                            arr[:, lanes], tiles[r], (((1,), (1,)), ((), ())),
                            preferred_element_type=jnp.float32,
                        )
                    return total

                acc = lax.fori_loop(0, piece // 2, multiply, acc)

    val[...] = jnp.dot(acc * sel[...], group[...], precision=lax.Precision.HIGHEST, preferred_element_type=jnp.float32)

    def value_copy(offset):
        to_rows = pl.ds(pl.multiple_of(lax.rem(inner + offset, INNER) * slots, slots), slots)
        return remote(val.at[to_rows], ret.at[own], v_send.at[offset], v_recv.at[offset], peer(offset))

    for offset in range(1, INNER):
        value_copy(offset).start()
    ret[own, :] = val[own, :]
    for offset in range(1, INNER):
        value_copy(offset).wait_recv()
    out[...] = jnp.dot(weights[...], ret[...], precision=lax.Precision.HIGHEST, preferred_element_type=jnp.float32)

    for offset in range(1, INNER):
        value_copy(offset).wait_send()
        for c in range(CHUNKS):
            print_copy(offset, c).wait_send()
    for k in range(outer_n - 1):
        for c in range(CHUNKS):
            @pl.when(jnp.logical_and(outer - k >= 0, has_right))
            def _():
                block_copy(outer - k, c, k, True).wait_send()

            @pl.when(jnp.logical_and(outer + k < outer_n, has_left))
            def _():
                block_copy(outer + k, c, k, False).wait_send()


def body(flux, coeff, diff_steps, footprint, tile_src, tile_local, tile_count):
    samples, rows, _ = flux.shape
    stations = footprint.shape[0]
    devices = lax.axis_size("station")
    outer_n = devices // INNER
    me = lax.axis_index("station")
    outer, inner = me // INNER, me % INNER
    slot_count = stations * KT
    cap = 2 * max(1, (slot_count + devices - 1) // devices)
    slots = outer_n * cap
    wide = samples * LANES_T

    flux_t = flux.reshape(samples, rows, TILES_DEV, TILE_LON).transpose(1, 0, 2, 3)
    flux_t = jnp.pad(flux_t, ((0, 0), (0, 0), (0, 1), (0, 0))).reshape(rows, wide, TILE_LON)
    coef_t = jnp.pad(coeff.reshape(rows, TILES_DEV, TILE_LON), ((0, 0), (0, 1), (0, 0)))
    gates = (jnp.arange(ITERS, dtype=jnp.int32)[:, None] < diff_steps[None, :]).astype(jnp.float32)

    order = jnp.arange(slot_count, dtype=jnp.int32)
    src = lax.dynamic_slice_in_dim(tile_src.reshape(devices, slot_count), outer * INNER, INNER, 0)
    loc = lax.dynamic_slice_in_dim(tile_local.reshape(devices, slot_count), outer * INNER, INNER, 0)
    target = src % INNER
    same = (target[:, :, None] == target[:, None, :]) & (order[None, :] < order[:, None])[None]
    rank = jnp.sum(same.astype(jnp.int32), axis=2)
    places = jnp.arange(slots, dtype=jnp.int32)
    my_target = lax.dynamic_index_in_dim(target, inner, 0, keepdims=False)
    my_rank = lax.dynamic_index_in_dim(rank, inner, 0, keepdims=False)
    place = my_target * slots + my_rank
    hot = place[None, :] == jnp.arange(INNER * slots, dtype=jnp.int32)[:, None]
    chosen = (target[:, None, :] == inner) & (rank[:, None, :] == places[None, :, None])
    code = (src // INNER) * LANES_T + loc + 1
    named = jnp.sum(jnp.where(chosen, code[:, None, :], 0), axis=2).reshape(INNER * slots) - 1
    columns = jnp.arange(outer_n * wide, dtype=jnp.int32)
    column_code = (columns // wide) * LANES_T + columns % LANES_T
    sel = (named[:, None] == column_code[None, :]).astype(jnp.float32)
    group = ((columns % wide) // LANES_T)[:, None] == jnp.arange(128, dtype=jnp.int32)[None, :]
    live = order % KT < tile_count[order // KT]
    mine = (order // KT)[None, :] == jnp.arange(stations, dtype=jnp.int32)[:, None]
    hits = (mine & live[None, :])[:, :, None] & (place[None, :, None] == jnp.arange(INNER * slots, dtype=jnp.int32)[None, None, :])
    weights = jnp.sum(hits.astype(jnp.float32), axis=1)

    ext = rows + 2 * ITERS
    vmem = pl.BlockSpec(memory_space=pltpu.VMEM)
    dma = pltpu.SemaphoreType.DMA
    observed = pl.pallas_call(
        functools.partial(kernel, outer_n, slots),
        out_shape=jax.ShapeDtypeStruct((stations, 128), jnp.float32),
        in_specs=[pl.BlockSpec(memory_space=pltpu.SMEM)] + [vmem] * 7,
        out_specs=vmem,
        scratch_shapes=[
            pltpu.VMEM((INNER * slots, footprint.shape[2]), jnp.bfloat16),
            pltpu.VMEM((INNER * slots, footprint.shape[2]), jnp.bfloat16),
            pltpu.VMEM((2, ITERS, wide, TILE_LON), jnp.bfloat16),
            pltpu.VMEM((2, ITERS, LANES_T, TILE_LON), jnp.float32),
            pltpu.VMEM((ext, wide, TILE_LON), jnp.float32),
            pltpu.VMEM((ext, wide, TILE_LON), jnp.float32),
            pltpu.VMEM((ext, LANES_T, TILE_LON), jnp.float32),
            pltpu.VMEM((rows, outer_n * wide, TILE_LON), jnp.bfloat16),
            pltpu.VMEM((INNER * slots, 128), jnp.float32),
            pltpu.VMEM((INNER * slots, 128), jnp.float32),
            dma((INNER, CHUNKS)), dma((INNER, CHUNKS)),
            dma((2, 2)), dma((2, 2)),
            dma((outer_n - 1, CHUNKS)), dma((outer_n - 1, CHUNKS)),
            dma((outer_n - 1, CHUNKS)), dma((outer_n - 1, CHUNKS)),
            dma((INNER,)), dma((INNER,)),
        ],
        compiler_params=pltpu.CompilerParams(
            collective_id=0, has_side_effects=True, vmem_limit_bytes=48 * 1024 * 1024
        ),
    )(
        gates, footprint.reshape(slot_count, footprint.shape[2]), hot.astype(jnp.bfloat16),
        flux_t, coef_t, sel, group.astype(jnp.float32), weights,
    )
    return lax.all_gather(observed[:, :samples], "sample", axis=1, tiled=True)


def solution(mesh):
    in_specs = (
        P("sample", "station", None),
        P("station", None),
        P("sample"),
        P("station", None, None),
        P(),
        P(),
        P("station"),
    )
    out_specs = P("station", None)
    return jax.shard_map(body, mesh=mesh, in_specs=in_specs, out_specs=out_specs, check_vma=False)
```

```python
import functools

import jax
import jax.numpy as jnp
from jax import lax
from jax.experimental import pallas as pl
from jax.experimental.pallas import tpu as pltpu
from jax.sharding import PartitionSpec as P

TILE_LON = 512
TILES_DEV = 7
LANES_T = 8
KT = 4
ITERS = 6
INNER = 8
CHUNKS = 4
PIECES = 8
GROUP_ROWS = 16
MESH = pl.DeviceIdType.MESH


def east_west(x, lane, tile):
    width = x.shape[1]
    west = pltpu.roll(x, 1, 1)
    first = west[:, :128]
    before = jnp.where(tile == 0, pltpu.roll(first, 2, 0), pltpu.roll(first, 1, 0))
    first = jnp.where(lane == 0, before, first)
    west = jnp.concatenate([first, west[:, 128:]], axis=1)
    east = pltpu.roll(x, width - 1, 1)
    last = east[:, width - 128 :]
    after = jnp.where(tile == TILES_DEV - 1, pltpu.roll(last, 6, 0), pltpu.roll(last, 7, 0))
    last = jnp.where(lane == 127, after, last)
    east = jnp.concatenate([east[:, : width - 128], last], axis=1)
    return west, east


def kernel(
    outer_n, slots, splits,
    gates, prints, hot, hot2, flux, coef, sel, sel2, group, weights, weights2,
    out,
    send, arr, send2, arr2, halo_f, halo_c, field_a, field_b, cof, tiles, acc, val, ret, val2, ret2,
    f_send, f_recv, g_send, g_recv, h_send, h_recv, r_send, r_recv, l_send, l_recv, v_send, v_recv, w_send, w_recv,
):
    rows = flux.shape[0]
    wide = flux.shape[1]
    samples = wide // LANES_T
    count = outer_n * INNER
    me = lax.axis_index("station")
    outer, inner = me // INNER, lax.rem(me, INNER)
    base = outer * INNER
    has_up, has_down = me > 0, me < count - 1
    has_left, has_right = outer > 0, outer < outer_n - 1
    first, last = outer == 0, outer == outer_n - 1
    is_end = jnp.logical_or(first, last)
    is_next = jnp.logical_or(outer == 1, outer == outer_n - 2)
    other_base = jnp.where(first, 1, jnp.where(last, outer_n - 2, jnp.where(outer == 1, 0, outer_n - 1))) * INNER
    lone_left = jnp.logical_and(outer >= 2, outer <= outer_n - 2)
    lone_right = jnp.logical_and(outer >= 1, outer <= outer_n - 3)
    lone_up = jnp.logical_and(lone_left, inner == 0)
    lone_down = jnp.logical_and(lone_right, inner == INNER - 1)

    def peer(offset):
        return base + lax.rem(inner + offset, INNER)

    def across(offset):
        return other_base + lax.rem(inner + offset, INNER)

    barrier = pltpu.get_barrier_semaphore()

    def greet(device):
        pl.semaphore_signal(barrier, inc=1, device_id={"station": device}, device_id_type=MESH)

    for offset in range(1, INNER):
        greet(peer(offset))
    others = ((lone_left, -INNER), (lone_right, INNER), (lone_up, -1), (lone_down, 1))
    for there, step in others:
        @pl.when(there)
        def _():
            greet(me + step)

    paired = jnp.logical_or(is_end, is_next)

    @pl.when(paired)
    def _():
        for offset in range(INNER):
            greet(across(offset))
    pl.semaphore_wait(
        barrier,
        INNER - 1 + sum(jnp.where(there, 1, 0) for there, _ in others) + jnp.where(paired, INNER, 0),
    )

    def remote(src, dst, ssem, rsem, device):
        return pltpu.make_async_remote_copy(
            src_ref=src, dst_ref=dst, send_sem=ssem, recv_sem=rsem,
            device_id={"station": device}, device_id_type=MESH,
        )

    def halo_copies(way):
        step = -1 if way == 0 else 1
        cut = pl.ds(0, ITERS) if way == 0 else pl.ds(rows - ITERS, ITERS)
        return (
            remote(flux.at[cut], halo_f.at[1 - way], h_send.at[way, 0], h_recv.at[1 - way, 0], me + step),
            remote(coef.at[cut], halo_c.at[1 - way], h_send.at[way, 1], h_recv.at[1 - way, 1], me + step),
        )

    for way, there in ((0, has_up), (1, has_down)):
        @pl.when(there)
        def _():
            for copy in halo_copies(way):
                copy.start()

        @pl.when(jnp.logical_not(there))
        def _():
            halo_f[way] = jnp.zeros(halo_f.shape[1:], halo_f.dtype)
            halo_c[way] = jnp.zeros(halo_c.shape[1:], halo_c.dtype)

    short = prints.shape[1] // splits
    own2 = pl.ds(pl.multiple_of(inner * GROUP_ROWS, GROUP_ROWS), GROUP_ROWS)

    def rows2(offset):
        return pl.ds(pl.multiple_of(lax.rem(inner + offset, INNER) * GROUP_ROWS, GROUP_ROWS), GROUP_ROWS)

    def group_copy(offset):
        return remote(send2.at[rows2(offset)], arr2.at[own2], g_send.at[offset], g_recv.at[offset], across(offset))

    @pl.when(is_end)
    def _():
        def pack2(i, carry):
            for j in range(2):
                at = i * 512 + j * 256
                stack = [prints[:, pl.ds(pl.multiple_of(q * short + at, 256), 256)] for q in range(splits)]
                packed = jnp.dot(hot2[...], jnp.concatenate(stack, axis=0), preferred_element_type=jnp.float32)
                send2[:, pl.ds(pl.multiple_of(at, 256), 256)] = packed.astype(jnp.bfloat16)
            return carry

        lax.fori_loop(0, short // 512, pack2, 0)
        for offset in range(INNER):
            group_copy(offset).start()
        missing = jnp.where(first, 1, outer_n - 2)

        def clear(r, carry):
            tiles[r, pl.ds(pl.multiple_of(missing * wide, wide), wide), :] = jnp.zeros((wide, TILE_LON), jnp.bfloat16)
            return carry

        lax.fori_loop(0, rows, clear, 0)

    length = prints.shape[1] // CHUNKS

    def print_copy(offset, c):
        target = peer(offset)
        lanes = pl.ds(c * length, length)
        to_rows = pl.ds(pl.multiple_of(lax.rem(inner + offset, INNER) * slots, slots), slots)
        my_rows = pl.ds(pl.multiple_of(inner * slots, slots), slots)
        return remote(send.at[to_rows, lanes], arr.at[my_rows, lanes], f_send.at[offset, c], f_recv.at[offset, c], target)

    for c in range(CHUNKS):
        def pack(i, carry):
            for j in range(4):
                lanes = pl.ds(pl.multiple_of(c * length + i * 1024 + j * 256, 256), 256)
                send[:, lanes] = jnp.dot(hot[...], prints[:, lanes], preferred_element_type=jnp.float32).astype(jnp.bfloat16)
            return carry

        lax.fori_loop(0, length // 1024, pack, 0)
        for offset in range(1, INNER):
            print_copy(offset, c).start()
    own = pl.ds(pl.multiple_of(inner * slots, slots), slots)
    arr[own, :] = send[own, :]

    def load(r, carry):
        field_a[r + ITERS] = flux[r].astype(jnp.float32)
        cof[r + ITERS] = coef[r]
        return carry

    lax.fori_loop(0, rows, load, 0)
    for way, there in ((0, has_up), (1, has_down)):
        @pl.when(there)
        def _():
            for copy in halo_copies(way):
                copy.wait_send()
            remote(flux.at[pl.ds(0, ITERS)], halo_f.at[way], h_send.at[way, 0], h_recv.at[way, 0], me).wait_recv()
            remote(coef.at[pl.ds(0, ITERS)], halo_c.at[way], h_send.at[way, 1], h_recv.at[way, 1], me).wait_recv()

    def load_halo(r, carry):
        field_a[r] = halo_f[0, r].astype(jnp.float32)
        cof[r] = halo_c[0, r]
        field_a[r + ITERS + rows] = halo_f[1, r].astype(jnp.float32)
        cof[r + ITERS + rows] = halo_c[1, r]
        return carry

    lax.fori_loop(0, ITERS, load_halo, 0)

    lane = lax.broadcasted_iota(jnp.int32, (LANES_T, 128), 1)
    tile = lax.broadcasted_iota(jnp.int32, (LANES_T, 128), 0)

    def updated(src, r, k, s):
        cut = slice(s * LANES_T, (s + 1) * LANES_T)
        center = src[r, cut, :]
        west, east = east_west(center, lane, tile)
        lap = src[r - 1, cut, :] + src[r + 1, cut, :] + west + east - 4.0 * center
        return center + gates[k, s] * cof[r] * lap

    src, dst = field_a, field_b
    for k in range(ITERS - 1):
        def row_pair(i, carry, src=src, dst=dst, k=k):
            for r in (k + 1 + 2 * i, k + 2 + 2 * i):
                for s in range(samples):
                    dst[r, s * LANES_T : (s + 1) * LANES_T, :] = updated(src, r, k, s)
            return carry

        lax.fori_loop(0, rows // 2 + ITERS - 1 - k, row_pair, 0)
        src, dst = dst, src

    piece = rows // PIECES

    def block_copy(block, c, k, to_right):
        at = tiles.at[pl.ds(c * piece, piece), pl.ds(pl.multiple_of(block * wide, wide), wide), :]
        if to_right:
            return remote(at, at, r_send.at[k, c], r_recv.at[k, c], me + INNER)
        return remote(at, at, l_send.at[k, c], l_recv.at[k, c], me - INNER)

    def goes(there, k, to_right):
        there = jnp.logical_and(there, has_right if to_right else has_left)
        if k == 0:
            there = jnp.logical_and(there, outer != (outer_n - 2 if to_right else 1))
        return there

    def start_block(block, c, k, to_right, there):
        @pl.when(goes(there, k, to_right))
        def _():
            block_copy(block, c, k, to_right).start()

    mine = pl.ds(pl.multiple_of(outer * wide, wide), wide)
    for c in range(PIECES):
        def last_pair(i, carry, src=src):
            for r in (c * piece + 2 * i, c * piece + 2 * i + 1):
                done = [updated(src, r + ITERS, ITERS - 1, s) for s in range(samples)]
                tiles[r, mine, :] = jnp.concatenate(done, axis=0).astype(jnp.bfloat16)
            return carry

        lax.fori_loop(0, piece // 2, last_pair, 0)
        start_block(outer, c, 0, True, has_right)
        start_block(outer, c, 0, False, has_left)

    def multiply(c):
        if c * CHUNKS % PIECES == 0:
            for offset in range(1, INNER):
                print_copy(offset, c * CHUNKS // PIECES).wait_recv()
        total = jnp.zeros(acc.shape, jnp.float32) if c == 0 else acc[...]
        for r in range(c * piece, (c + 1) * piece):
            total = total + lax.dot_general(
                arr[:, r * TILE_LON : (r + 1) * TILE_LON], tiles[r], (((1,), (1,)), ((), ())),
                preferred_element_type=jnp.float32,
            )
        acc[...] = total

    def value_copy2(offset):
        return remote(val2.at[rows2(offset)], ret2.at[own2], w_send.at[offset], w_recv.at[offset], across(offset))

    def group_values():
        for offset in range(INNER):
            group_copy(offset).wait_recv()
        per_split = rows // splits
        total = jnp.zeros(sel2.shape[1:], jnp.float32)
        for q in range(splits):
            def add_row(r, part, q=q):
                return part + lax.dot_general(
                    arr2[:, pl.ds(pl.multiple_of(r * TILE_LON, TILE_LON), TILE_LON)],
                    tiles[q * per_split + r, mine, :], (((1,), (1,)), ((), ())),
                    preferred_element_type=jnp.float32,
                )

            part = jnp.zeros(sel2.shape[1:], jnp.float32)
            for r in range(per_split):
                part = add_row(r, part)
            total = total + part * sel2[q]
        val2[...] = jnp.dot(total, group[:wide, :], precision=lax.Precision.HIGHEST, preferred_element_type=jnp.float32)
        for offset in range(INNER):
            value_copy2(offset).start()

    for k in range(outer_n - 1):
        from_left, from_right = outer - 1 - k >= 0, outer + 1 + k < outer_n
        if k == 0:
            from_left = jnp.logical_and(from_left, jnp.logical_not(last))
            from_right = jnp.logical_and(from_right, jnp.logical_not(first))
        for c in range(PIECES):
            @pl.when(from_left)
            def _():
                block_copy(outer - 1 - k, c, k, True).wait_recv()

            if k < outer_n - 2:
                start_block(outer - 1 - k, c, k + 1, True, from_left)

            @pl.when(from_right)
            def _():
                block_copy(outer + 1 + k, c, k, False).wait_recv()

            if k < outer_n - 2:
                start_block(outer + 1 + k, c, k + 1, False, from_right)

            if k >= outer_n - 3:
                @pl.when(is_end if k == outer_n - 2 else jnp.logical_not(is_end))
                def _():
                    multiply(c)

        if k == 0:
            pl.when(is_next)(group_values)

    val[...] = jnp.dot(acc[...] * sel[...], group[...], precision=lax.Precision.HIGHEST, preferred_element_type=jnp.float32)

    def value_copy(offset):
        to_rows = pl.ds(pl.multiple_of(lax.rem(inner + offset, INNER) * slots, slots), slots)
        return remote(val.at[to_rows], ret.at[own], v_send.at[offset], v_recv.at[offset], peer(offset))

    for offset in range(1, INNER):
        value_copy(offset).start()
    ret[own, :] = val[own, :]
    for offset in range(1, INNER):
        value_copy(offset).wait_recv()
    out[...] = jnp.dot(weights[...], ret[...], precision=lax.Precision.HIGHEST, preferred_element_type=jnp.float32)

    @pl.when(is_end)
    def _():
        for offset in range(INNER):
            value_copy2(offset).wait_recv()
        out[...] += jnp.dot(weights2[...], ret2[...], precision=lax.Precision.HIGHEST, preferred_element_type=jnp.float32)
        for offset in range(INNER):
            group_copy(offset).wait_send()

    @pl.when(is_next)
    def _():
        for offset in range(INNER):
            value_copy2(offset).wait_send()

    for offset in range(1, INNER):
        value_copy(offset).wait_send()
        for c in range(CHUNKS):
            print_copy(offset, c).wait_send()
    for k in range(outer_n - 1):
        for c in range(PIECES):
            @pl.when(goes(outer - k >= 0, k, True))
            def _():
                block_copy(outer - k, c, k, True).wait_send()

            @pl.when(goes(outer + k < outer_n, k, False))
            def _():
                block_copy(outer + k, c, k, False).wait_send()


def body(flux, coeff, diff_steps, footprint, tile_src, tile_local, tile_count):
    samples, rows, _ = flux.shape
    stations = footprint.shape[0]
    devices = lax.axis_size("station")
    outer_n = devices // INNER
    me = lax.axis_index("station")
    outer, inner = me // INNER, me % INNER
    slot_count = stations * KT
    cap = 2 * max(1, (slot_count + devices - 1) // devices)
    slots = outer_n * cap
    wide = samples * LANES_T

    flux_t = flux.reshape(samples, rows, TILES_DEV, TILE_LON).transpose(1, 0, 2, 3)
    flux_t = jnp.pad(flux_t, ((0, 0), (0, 0), (0, 1), (0, 0))).reshape(rows, wide, TILE_LON)
    coef_t = jnp.pad(coeff.reshape(rows, TILES_DEV, TILE_LON), ((0, 0), (0, 1), (0, 0)))
    gates = (jnp.arange(ITERS, dtype=jnp.int32)[:, None] < diff_steps[None, :]).astype(jnp.float32)

    order = jnp.arange(slot_count, dtype=jnp.int32)
    src = lax.dynamic_slice_in_dim(tile_src.reshape(devices, slot_count), outer * INNER, INNER, 0)
    loc = lax.dynamic_slice_in_dim(tile_local.reshape(devices, slot_count), outer * INNER, INNER, 0)
    target = src % INNER
    band_layer = src // INNER
    beside = jnp.where(outer == 0, 1, jnp.where(outer == outer_n - 1, outer_n - 2, -1))
    grouped = band_layer == beside
    target = jnp.where(grouped, INNER + target, target)
    same = (target[:, :, None] == target[:, None, :]) & (order[None, :] < order[:, None])[None]
    rank = jnp.sum(same.astype(jnp.int32), axis=2)
    places = jnp.arange(slots, dtype=jnp.int32)
    my_target = lax.dynamic_index_in_dim(target, inner, 0, keepdims=False)
    my_rank = lax.dynamic_index_in_dim(rank, inner, 0, keepdims=False)
    place = jnp.where(my_target < INNER, my_target * slots + my_rank, -1)
    hot = place[None, :] == jnp.arange(INNER * slots, dtype=jnp.int32)[:, None]
    splits = GROUP_ROWS // cap
    group_rows = jnp.arange(INNER * GROUP_ROWS, dtype=jnp.int32)
    row_owner, row_split, row_slot = group_rows // GROUP_ROWS, group_rows % GROUP_ROWS // cap, group_rows % cap
    in_group = (my_target[None, :] == INNER + row_owner[:, None]) & (my_rank[None, :] == row_slot[:, None])
    hot2 = in_group[:, None, :] & (row_split[:, None] == jnp.arange(splits, dtype=jnp.int32)[None, :])[:, :, None]
    hot2 = hot2.reshape(INNER * GROUP_ROWS, splits * slot_count)
    from_layer = jnp.where(outer == 1, 0, outer_n - 1)
    src_end = lax.dynamic_slice_in_dim(tile_src.reshape(devices, slot_count), from_layer * INNER, INNER, 0)
    loc_end = lax.dynamic_slice_in_dim(tile_local.reshape(devices, slot_count), from_layer * INNER, INNER, 0)
    to_me = src_end == me
    rank_end = jnp.sum((to_me[:, None, :] & (order[None, :] < order[:, None])[None]).astype(jnp.int32), axis=2)
    taken = to_me[:, None, :] & (rank_end[:, None, :] == jnp.arange(cap, dtype=jnp.int32)[None, :, None])
    tile_end = jnp.sum(jnp.where(taken, loc_end[:, None, :] + 1, 0), axis=2) - 1
    tile_end = jnp.broadcast_to(tile_end[:, None, :], (INNER, splits, cap)).reshape(INNER * GROUP_ROWS)
    sel2 = (tile_end[None, :, None] == (jnp.arange(wide, dtype=jnp.int32) % LANES_T)[None, None, :]) & (
        row_split[None, :, None] == jnp.arange(splits, dtype=jnp.int32)[:, None, None]
    )
    chosen = (target[:, None, :] == inner) & (rank[:, None, :] == places[None, :, None])
    code = band_layer * LANES_T + loc + 1
    named = jnp.sum(jnp.where(chosen, code[:, None, :], 0), axis=2).reshape(INNER * slots) - 1
    columns = jnp.arange(outer_n * wide, dtype=jnp.int32)
    column_code = (columns // wide) * LANES_T + columns % LANES_T
    sel = (named[:, None] == column_code[None, :]).astype(jnp.float32)
    group = ((columns % wide) // LANES_T)[:, None] == jnp.arange(128, dtype=jnp.int32)[None, :]
    live = order % KT < tile_count[order // KT]
    mine = (order // KT)[None, :] == jnp.arange(stations, dtype=jnp.int32)[:, None]
    hits = (mine & live[None, :])[:, :, None] & (place[None, :, None] == jnp.arange(INNER * slots, dtype=jnp.int32)[None, None, :])
    weights = jnp.sum(hits.astype(jnp.float32), axis=1)
    weights2 = jnp.sum(((mine & live[None, :])[:, None, :] & in_group[None]).astype(jnp.float32), axis=2)

    ext = rows + 2 * ITERS
    vmem = pl.BlockSpec(memory_space=pltpu.VMEM)
    dma = pltpu.SemaphoreType.DMA
    observed = pl.pallas_call(
        functools.partial(kernel, outer_n, slots, splits),
        out_shape=jax.ShapeDtypeStruct((stations, 128), jnp.float32),
        in_specs=[pl.BlockSpec(memory_space=pltpu.SMEM)] + [vmem] * 10,
        out_specs=vmem,
        scratch_shapes=[
            pltpu.VMEM((INNER * slots, footprint.shape[2]), jnp.bfloat16),
            pltpu.VMEM((INNER * slots, footprint.shape[2]), jnp.bfloat16),
            pltpu.VMEM((INNER * GROUP_ROWS, footprint.shape[2] // splits), jnp.bfloat16),
            pltpu.VMEM((INNER * GROUP_ROWS, footprint.shape[2] // splits), jnp.bfloat16),
            pltpu.VMEM((2, ITERS, wide, TILE_LON), jnp.bfloat16),
            pltpu.VMEM((2, ITERS, LANES_T, TILE_LON), jnp.float32),
            pltpu.VMEM((ext, wide, TILE_LON), jnp.float32),
            pltpu.VMEM((ext, wide, TILE_LON), jnp.float32),
            pltpu.VMEM((ext, LANES_T, TILE_LON), jnp.float32),
            pltpu.VMEM((rows, outer_n * wide, TILE_LON), jnp.bfloat16),
            pltpu.VMEM((INNER * slots, outer_n * wide), jnp.float32),
            pltpu.VMEM((INNER * slots, 128), jnp.float32),
            pltpu.VMEM((INNER * slots, 128), jnp.float32),
            pltpu.VMEM((INNER * GROUP_ROWS, 128), jnp.float32),
            pltpu.VMEM((INNER * GROUP_ROWS, 128), jnp.float32),
            dma((INNER, CHUNKS)), dma((INNER, CHUNKS)),
            dma((INNER,)), dma((INNER,)),
            dma((2, 2)), dma((2, 2)),
            dma((outer_n - 1, PIECES)), dma((outer_n - 1, PIECES)),
            dma((outer_n - 1, PIECES)), dma((outer_n - 1, PIECES)),
            dma((INNER,)), dma((INNER,)),
            dma((INNER,)), dma((INNER,)),
        ],
        compiler_params=pltpu.CompilerParams(
            collective_id=0, has_side_effects=True, vmem_limit_bytes=50 * 1024 * 1024
        ),
    )(
        gates, footprint.reshape(slot_count, footprint.shape[2]), hot.astype(jnp.bfloat16),
        hot2.astype(jnp.bfloat16), flux_t, coef_t, sel, sel2.astype(jnp.float32), group.astype(jnp.float32),
        weights, weights2,
    )
    return lax.all_gather(observed[:, :samples], "sample", axis=1, tiled=True)


def solution(mesh):
    in_specs = (
        P("sample", "station", None),
        P("station", None),
        P("sample"),
        P("station", None, None),
        P(),
        P(),
        P("station"),
    )
    out_specs = P("station", None)
    return jax.shard_map(body, mesh=mesh, in_specs=in_specs, out_specs=out_specs, check_vma=False)
```

```python
import functools

import jax
import jax.numpy as jnp
from jax import lax
from jax.experimental import pallas as pl
from jax.experimental.pallas import tpu as pltpu
from jax.sharding import PartitionSpec as P

TILE_LON = 512
TILES_DEV = 7
LANES_T = 8
KT = 4
ITERS = 6
INNER = 8
PIECES = 8
GROUP_ROWS = 16
MESH = pl.DeviceIdType.MESH


def east_west(x, lane, tile):
    width = x.shape[1]
    west = pltpu.roll(x, 1, 1)
    first = west[:, :128]
    before = jnp.where(tile == 0, pltpu.roll(first, 2, 0), pltpu.roll(first, 1, 0))
    first = jnp.where(lane == 0, before, first)
    west = jnp.concatenate([first, west[:, 128:]], axis=1)
    east = pltpu.roll(x, width - 1, 1)
    last = east[:, width - 128 :]
    after = jnp.where(tile == TILES_DEV - 1, pltpu.roll(last, 6, 0), pltpu.roll(last, 7, 0))
    last = jnp.where(lane == 127, after, last)
    east = jnp.concatenate([east[:, : width - 128], last], axis=1)
    return west, east


def kernel(
    outer_n, slots, splits,
    steps, prints, hot, hot2, flux, coef, sel, sel2, group, weights, weights2,
    out,
    send, arr, send2, arr2, halo_f, halo_c, field_a, field_b, cof, tiles, acc, val, ret, val2, ret2,
    f_send, f_recv, g_send, g_recv, h_send, h_recv, r_send, r_recv, l_send, l_recv, v_send, v_recv, w_send, w_recv,
):
    rows = flux.shape[0]
    wide = flux.shape[1]
    samples = wide // LANES_T
    count = outer_n * INNER
    me = lax.axis_index("station")
    outer, inner = me // INNER, lax.rem(me, INNER)
    base = outer * INNER
    has_up, has_down = me > 0, me < count - 1
    has_left, has_right = outer > 0, outer < outer_n - 1
    first, last = outer == 0, outer == outer_n - 1
    is_end = jnp.logical_or(first, last)
    is_next = jnp.logical_or(outer == 1, outer == outer_n - 2)
    other_base = jnp.where(first, 1, jnp.where(last, outer_n - 2, jnp.where(outer == 1, 0, outer_n - 1))) * INNER
    lone_left = jnp.logical_and(outer >= 2, outer <= outer_n - 2)
    lone_right = jnp.logical_and(outer >= 1, outer <= outer_n - 3)
    lone_up = jnp.logical_and(lone_left, inner == 0)
    lone_down = jnp.logical_and(lone_right, inner == INNER - 1)

    def peer(offset):
        return base + lax.rem(inner + offset, INNER)

    def across(offset):
        return other_base + lax.rem(inner + offset, INNER)

    barrier = pltpu.get_barrier_semaphore()

    def greet(device):
        pl.semaphore_signal(barrier, inc=1, device_id={"station": device}, device_id_type=MESH)

    for offset in range(1, INNER):
        greet(peer(offset))
    others = ((lone_left, -INNER), (lone_right, INNER), (lone_up, -1), (lone_down, 1))
    for there, step in others:
        @pl.when(there)
        def _():
            greet(me + step)

    paired = jnp.logical_or(is_end, is_next)

    @pl.when(paired)
    def _():
        for offset in range(INNER):
            greet(across(offset))
    pl.semaphore_wait(
        barrier,
        INNER - 1 + sum(jnp.where(there, 1, 0) for there, _ in others) + jnp.where(paired, INNER, 0),
    )

    def remote(src, dst, ssem, rsem, device):
        return pltpu.make_async_remote_copy(
            src_ref=src, dst_ref=dst, send_sem=ssem, recv_sem=rsem,
            device_id={"station": device}, device_id_type=MESH,
        )

    def halo_copies(way):
        step = -1 if way == 0 else 1
        cut = pl.ds(0, ITERS) if way == 0 else pl.ds(rows - ITERS, ITERS)
        return (
            remote(flux.at[cut], halo_f.at[1 - way], h_send.at[way, 0], h_recv.at[1 - way, 0], me + step),
            remote(coef.at[cut], halo_c.at[1 - way], h_send.at[way, 1], h_recv.at[1 - way, 1], me + step),
        )

    for way, there in ((0, has_up), (1, has_down)):
        @pl.when(there)
        def _():
            for copy in halo_copies(way):
                copy.start()

        @pl.when(jnp.logical_not(there))
        def _():
            halo_f[way] = jnp.zeros(halo_f.shape[1:], halo_f.dtype)
            halo_c[way] = jnp.zeros(halo_c.shape[1:], halo_c.dtype)

    cells = prints.shape[2]
    short = cells // splits

    def some_prints(at):
        block = prints[:, :, pl.ds(pl.multiple_of(at, 256), 256)]
        return block.reshape(block.shape[0] * KT, 256)

    own2 = pl.ds(pl.multiple_of(inner * GROUP_ROWS, GROUP_ROWS), GROUP_ROWS)

    def rows2(offset):
        return pl.ds(pl.multiple_of(lax.rem(inner + offset, INNER) * GROUP_ROWS, GROUP_ROWS), GROUP_ROWS)

    def group_copy(offset):
        return remote(send2.at[rows2(offset)], arr2.at[own2], g_send.at[offset], g_recv.at[offset], across(offset))

    @pl.when(is_end)
    def _():
        def pack2(i, carry):
            for j in range(2):
                at = i * 512 + j * 256
                stack = [some_prints(q * short + at) for q in range(splits)]
                packed = jnp.dot(hot2[...], jnp.concatenate(stack, axis=0), preferred_element_type=jnp.float32)
                send2[:, pl.ds(pl.multiple_of(at, 256), 256)] = packed.astype(jnp.bfloat16)
            return carry

        lax.fori_loop(0, short // 512, pack2, 0)
        for offset in range(INNER):
            group_copy(offset).start()
        missing = jnp.where(first, 1, outer_n - 2)

        def clear(r, carry):
            tiles[r, pl.ds(pl.multiple_of(missing * wide, wide), wide), :] = jnp.zeros((wide, TILE_LON), jnp.bfloat16)
            return carry

        lax.fori_loop(0, rows, clear, 0)

    length = cells // PIECES

    def print_copy(offset, c):
        target = peer(offset)
        lanes = pl.ds(pl.multiple_of(c * length, length), length)
        to_rows = pl.ds(pl.multiple_of(lax.rem(inner + offset, INNER) * slots, slots), slots)
        my_rows = pl.ds(pl.multiple_of(inner * slots, slots), slots)
        return remote(send.at[to_rows, lanes], arr.at[my_rows, lanes], f_send.at[offset, c], f_recv.at[offset, c], target)

    own = pl.ds(pl.multiple_of(inner * slots, slots), slots)

    def send_prints(c):
        for j in range(length // 256):
            at = c * length + j * 256
            packed = jnp.dot(hot[...], some_prints(at), preferred_element_type=jnp.float32)
            send[:, pl.ds(pl.multiple_of(at, 256), 256)] = packed.astype(jnp.bfloat16)
        for offset in range(1, INNER):
            print_copy(offset, c).start()

    def load(r, carry):
        field_a[r + ITERS] = flux[r].astype(jnp.float32)
        cof[r + ITERS] = coef[r]
        return carry

    lax.fori_loop(0, rows, load, 0)
    for way, there in ((0, has_up), (1, has_down)):
        @pl.when(there)
        def _():
            for copy in halo_copies(way):
                copy.wait_send()
            remote(flux.at[pl.ds(0, ITERS)], halo_f.at[way], h_send.at[way, 0], h_recv.at[way, 0], me).wait_recv()
            remote(coef.at[pl.ds(0, ITERS)], halo_c.at[way], h_send.at[way, 1], h_recv.at[way, 1], me).wait_recv()

    def load_halo(r, carry):
        field_a[r] = halo_f[0, r].astype(jnp.float32)
        cof[r] = halo_c[0, r]
        field_a[r + ITERS + rows] = halo_f[1, r].astype(jnp.float32)
        cof[r + ITERS + rows] = halo_c[1, r]
        return carry

    lax.fori_loop(0, ITERS, load_halo, 0)

    lane = lax.broadcasted_iota(jnp.int32, (LANES_T, 128), 1)
    tile = lax.broadcasted_iota(jnp.int32, (LANES_T, 128), 0)

    def updated(src, r, k, s):
        cut = slice(s * LANES_T, (s + 1) * LANES_T)
        center = src[r, cut, :]
        west, east = east_west(center, lane, tile)
        lap = src[r - 1, cut, :] + src[r + 1, cut, :] + west + east - 4.0 * center
        return center + jnp.where(k < steps[s], 1.0, 0.0) * cof[r] * lap

    piece = rows // PIECES

    def block_copy(block, c, k, to_right):
        at = tiles.at[pl.ds(c * piece, piece), pl.ds(pl.multiple_of(block * wide, wide), wide), :]
        if to_right:
            return remote(at, at, r_send.at[k, c], r_recv.at[k, c], me + INNER)
        return remote(at, at, l_send.at[k, c], l_recv.at[k, c], me - INNER)

    def goes(there, k, to_right):
        there = jnp.logical_and(there, has_right if to_right else has_left)
        if k == 0:
            there = jnp.logical_and(there, outer != (outer_n - 2 if to_right else 1))
        return there

    def start_block(block, c, k, to_right, there):
        @pl.when(goes(there, k, to_right))
        def _():
            block_copy(block, c, k, to_right).start()

    mine = pl.ds(pl.multiple_of(outer * wide, wide), wide)

    def step_row(r, k):
        src, dst = (field_a, field_b) if k % 2 == 0 else (field_b, field_a)
        done = [updated(src, r, k, s) for s in range(samples)]
        if k == ITERS - 1:
            tiles[r - ITERS, mine, :] = jnp.concatenate(done, axis=0).astype(jnp.bfloat16)
        else:
            for s in range(samples):
                dst[r, s * LANES_T : (s + 1) * LANES_T, :] = done[s]

    def send_piece(c):
        start_block(outer, c, 0, True, has_right)
        start_block(outer, c, 0, False, has_left)

    for k in range(ITERS):
        def row_pair(i, carry, k=k):
            step_row(k + 1 + 2 * i, k)
            step_row(k + 2 + 2 * i, k)
            return carry

        lax.fori_loop(0, piece // 2 + ITERS - 1 - k, row_pair, 0)
    send_piece(0)
    send_prints(0)

    def next_piece(c, carry):
        for k in range(ITERS):
            for j in range(piece):
                step_row(c * piece + 2 * ITERS - 1 - k + j, k)
        send_piece(c)
        send_prints(c)
        return carry

    lax.fori_loop(1, PIECES, next_piece, 0)
    arr[own, :] = send[own, :]

    def multiply(c):
        for offset in range(1, INNER):
            print_copy(offset, c).wait_recv()
        total = jnp.zeros(acc.shape, jnp.float32) if c == 0 else acc[...]
        for r in range(c * piece, (c + 1) * piece):
            total = total + lax.dot_general(
                arr[:, r * TILE_LON : (r + 1) * TILE_LON], tiles[r], (((1,), (1,)), ((), ())),
                preferred_element_type=jnp.float32,
            )
        acc[...] = total

    def value_copy2(offset):
        return remote(val2.at[rows2(offset)], ret2.at[own2], w_send.at[offset], w_recv.at[offset], across(offset))

    def group_values():
        for offset in range(INNER):
            group_copy(offset).wait_recv()
        per_split = rows // splits
        total = jnp.zeros(sel2.shape[1:], jnp.float32)
        for q in range(splits):
            def add_row(r, part, q=q):
                return part + lax.dot_general(
                    arr2[:, pl.ds(pl.multiple_of(r * TILE_LON, TILE_LON), TILE_LON)],
                    tiles[q * per_split + r, mine, :], (((1,), (1,)), ((), ())),
                    preferred_element_type=jnp.float32,
                )

            part = jnp.zeros(sel2.shape[1:], jnp.float32)
            for r in range(per_split):
                part = add_row(r, part)
            total = total + part * sel2[q]
        val2[...] = jnp.dot(total, group[:wide, :], precision=lax.Precision.HIGHEST, preferred_element_type=jnp.float32)
        for offset in range(INNER):
            value_copy2(offset).start()

    for k in range(outer_n - 1):
        from_left, from_right = outer - 1 - k >= 0, outer + 1 + k < outer_n
        if k == 0:
            from_left = jnp.logical_and(from_left, jnp.logical_not(last))
            from_right = jnp.logical_and(from_right, jnp.logical_not(first))
        for c in range(PIECES):
            @pl.when(from_left)
            def _():
                block_copy(outer - 1 - k, c, k, True).wait_recv()

            if k < outer_n - 2:
                start_block(outer - 1 - k, c, k + 1, True, from_left)

            @pl.when(from_right)
            def _():
                block_copy(outer + 1 + k, c, k, False).wait_recv()

            if k < outer_n - 2:
                start_block(outer + 1 + k, c, k + 1, False, from_right)

            if k >= outer_n - 3:
                @pl.when(is_end if k == outer_n - 2 else jnp.logical_not(is_end))
                def _():
                    multiply(c)

        if k == 0:
            pl.when(is_next)(group_values)

    val[...] = jnp.dot(acc[...] * sel[...], group[...], precision=lax.Precision.HIGHEST, preferred_element_type=jnp.float32)

    def value_copy(offset):
        to_rows = pl.ds(pl.multiple_of(lax.rem(inner + offset, INNER) * slots, slots), slots)
        return remote(val.at[to_rows], ret.at[own], v_send.at[offset], v_recv.at[offset], peer(offset))

    for offset in range(1, INNER):
        value_copy(offset).start()
    ret[own, :] = val[own, :]
    for offset in range(1, INNER):
        value_copy(offset).wait_recv()
    out[...] = jnp.dot(weights[...], ret[...], precision=lax.Precision.HIGHEST, preferred_element_type=jnp.float32)

    @pl.when(is_end)
    def _():
        for offset in range(INNER):
            value_copy2(offset).wait_recv()
        out[...] += jnp.dot(weights2[...], ret2[...], precision=lax.Precision.HIGHEST, preferred_element_type=jnp.float32)
        for offset in range(INNER):
            group_copy(offset).wait_send()

    @pl.when(is_next)
    def _():
        for offset in range(INNER):
            value_copy2(offset).wait_send()

    for offset in range(1, INNER):
        value_copy(offset).wait_send()
        for c in range(PIECES):
            print_copy(offset, c).wait_send()
    for k in range(outer_n - 1):
        for c in range(PIECES):
            @pl.when(goes(outer - k >= 0, k, True))
            def _():
                block_copy(outer - k, c, k, True).wait_send()

            @pl.when(goes(outer + k < outer_n, k, False))
            def _():
                block_copy(outer + k, c, k, False).wait_send()


def body(flux, coeff, diff_steps, footprint, tile_src, tile_local, tile_count):
    samples, rows, _ = flux.shape
    stations = footprint.shape[0]
    devices = lax.axis_size("station")
    outer_n = devices // INNER
    me = lax.axis_index("station")
    outer, inner = me // INNER, me % INNER
    slot_count = stations * KT
    cap = 2 * max(1, (slot_count + devices - 1) // devices)
    slots = outer_n * cap
    wide = samples * LANES_T

    flux_t = flux.reshape(samples, rows, TILES_DEV, TILE_LON).transpose(1, 0, 2, 3)
    flux_t = jnp.pad(flux_t, ((0, 0), (0, 0), (0, 1), (0, 0))).reshape(rows, wide, TILE_LON)
    coef_t = jnp.pad(coeff.reshape(rows, TILES_DEV, TILE_LON), ((0, 0), (0, 1), (0, 0)))

    order = jnp.arange(slot_count, dtype=jnp.int32)
    listed = (tile_src[:, :, 0] * LANES_T + tile_local).reshape(devices, slot_count)
    here = lax.dynamic_slice_in_dim(listed, outer * INNER, INNER, 0)
    src, loc = here // LANES_T, here % LANES_T
    target = src % INNER
    band_layer = src // INNER
    beside = jnp.where(outer == 0, 1, jnp.where(outer == outer_n - 1, outer_n - 2, -1))
    grouped = band_layer == beside
    target = jnp.where(grouped, INNER + target, target)
    same = (target[:, :, None] == target[:, None, :]) & (order[None, :] < order[:, None])[None]
    rank = jnp.sum(same.astype(jnp.int32), axis=2)
    places = jnp.arange(slots, dtype=jnp.int32)
    my_target = lax.dynamic_index_in_dim(target, inner, 0, keepdims=False)
    my_rank = lax.dynamic_index_in_dim(rank, inner, 0, keepdims=False)
    place = jnp.where(my_target < INNER, my_target * slots + my_rank, -1)
    hot = place[None, :] == jnp.arange(INNER * slots, dtype=jnp.int32)[:, None]
    splits = GROUP_ROWS // cap
    group_rows = jnp.arange(INNER * GROUP_ROWS, dtype=jnp.int32)
    row_owner, row_split, row_slot = group_rows // GROUP_ROWS, group_rows % GROUP_ROWS // cap, group_rows % cap
    in_group = (my_target[None, :] == INNER + row_owner[:, None]) & (my_rank[None, :] == row_slot[:, None])
    hot2 = in_group[:, None, :] & (row_split[:, None] == jnp.arange(splits, dtype=jnp.int32)[None, :])[:, :, None]
    hot2 = hot2.reshape(INNER * GROUP_ROWS, splits * slot_count)
    from_layer = jnp.where(outer == 1, 0, outer_n - 1)
    there = lax.dynamic_slice_in_dim(listed, from_layer * INNER, INNER, 0)
    src_end, loc_end = there // LANES_T, there % LANES_T
    to_me = src_end == me
    rank_end = jnp.sum((to_me[:, None, :] & (order[None, :] < order[:, None])[None]).astype(jnp.int32), axis=2)
    taken = to_me[:, None, :] & (rank_end[:, None, :] == jnp.arange(cap, dtype=jnp.int32)[None, :, None])
    tile_end = jnp.sum(jnp.where(taken, loc_end[:, None, :] + 1, 0), axis=2) - 1
    tile_end = jnp.broadcast_to(tile_end[:, None, :], (INNER, splits, cap)).reshape(INNER * GROUP_ROWS)
    sel2 = (tile_end[None, :, None] == (jnp.arange(wide, dtype=jnp.int32) % LANES_T)[None, None, :]) & (
        row_split[None, :, None] == jnp.arange(splits, dtype=jnp.int32)[:, None, None]
    )
    chosen = (target[:, None, :] == inner) & (rank[:, None, :] == places[None, :, None])
    code = band_layer * LANES_T + loc + 1
    named = jnp.sum(jnp.where(chosen, code[:, None, :], 0), axis=2).reshape(INNER * slots) - 1
    columns = jnp.arange(outer_n * wide, dtype=jnp.int32)
    column_code = (columns // wide) * LANES_T + columns % LANES_T
    sel = (named[:, None] == column_code[None, :]).astype(jnp.float32)
    group = ((columns % wide) // LANES_T)[:, None] == jnp.arange(128, dtype=jnp.int32)[None, :]
    live = (jnp.arange(KT, dtype=jnp.int32)[None, :] < tile_count[:, None]).reshape(slot_count)
    mine = (order // KT)[None, :] == jnp.arange(stations, dtype=jnp.int32)[:, None]
    hits = (mine & live[None, :])[:, :, None] & (place[None, :, None] == jnp.arange(INNER * slots, dtype=jnp.int32)[None, None, :])
    weights = jnp.sum(hits.astype(jnp.float32), axis=1)
    weights2 = jnp.sum(((mine & live[None, :])[:, None, :] & in_group[None]).astype(jnp.float32), axis=2)

    ext = rows + 2 * ITERS
    vmem = pl.BlockSpec(memory_space=pltpu.VMEM)
    dma = pltpu.SemaphoreType.DMA
    observed = pl.pallas_call(
        functools.partial(kernel, outer_n, slots, splits),
        out_shape=jax.ShapeDtypeStruct((stations, 128), jnp.float32),
        in_specs=[pl.BlockSpec(memory_space=pltpu.SMEM)] + [vmem] * 10,
        out_specs=vmem,
        scratch_shapes=[
            pltpu.VMEM((INNER * slots, footprint.shape[2]), jnp.bfloat16),
            pltpu.VMEM((INNER * slots, footprint.shape[2]), jnp.bfloat16),
            pltpu.VMEM((INNER * GROUP_ROWS, footprint.shape[2] // splits), jnp.bfloat16),
            pltpu.VMEM((INNER * GROUP_ROWS, footprint.shape[2] // splits), jnp.bfloat16),
            pltpu.VMEM((2, ITERS, wide, TILE_LON), jnp.bfloat16),
            pltpu.VMEM((2, ITERS, LANES_T, TILE_LON), jnp.float32),
            pltpu.VMEM((ext, wide, TILE_LON), jnp.float32),
            pltpu.VMEM((ext, wide, TILE_LON), jnp.float32),
            pltpu.VMEM((ext, LANES_T, TILE_LON), jnp.float32),
            pltpu.VMEM((rows, outer_n * wide, TILE_LON), jnp.bfloat16),
            pltpu.VMEM((INNER * slots, outer_n * wide), jnp.float32),
            pltpu.VMEM((INNER * slots, 128), jnp.float32),
            pltpu.VMEM((INNER * slots, 128), jnp.float32),
            pltpu.VMEM((INNER * GROUP_ROWS, 128), jnp.float32),
            pltpu.VMEM((INNER * GROUP_ROWS, 128), jnp.float32),
            dma((INNER, PIECES)), dma((INNER, PIECES)),
            dma((INNER,)), dma((INNER,)),
            dma((2, 2)), dma((2, 2)),
            dma((outer_n - 1, PIECES)), dma((outer_n - 1, PIECES)),
            dma((outer_n - 1, PIECES)), dma((outer_n - 1, PIECES)),
            dma((INNER,)), dma((INNER,)),
            dma((INNER,)), dma((INNER,)),
        ],
        compiler_params=pltpu.CompilerParams(
            collective_id=0, has_side_effects=True, vmem_limit_bytes=50 * 1024 * 1024
        ),
    )(
        diff_steps, footprint, hot.astype(jnp.bfloat16),
        hot2.astype(jnp.bfloat16), flux_t, coef_t, sel, sel2.astype(jnp.float32), group.astype(jnp.float32),
        weights, weights2,
    )
    return lax.all_gather(observed[:, :samples], "sample", axis=1, tiled=True)


def solution(mesh):
    in_specs = (
        P("sample", "station", None),
        P("station", None),
        P("sample"),
        P("station", None, None),
        P(),
        P(),
        P("station"),
    )
    out_specs = P("station", None)
    return jax.shard_map(body, mesh=mesh, in_specs=in_specs, out_specs=out_specs, check_vma=False)
```

```python
import functools

import jax
import jax.numpy as jnp
from jax import lax
from jax.experimental import pallas as pl
from jax.experimental.pallas import tpu as pltpu
from jax.sharding import PartitionSpec as P

TILE_LON = 512
TILES_DEV = 7
LANES_T = 8
KT = 4
ITERS = 6
INNER = 8
PIECES = 8
AHEAD = 3
GROUP_ROWS = 16
MESH = pl.DeviceIdType.MESH


def east_west(x, lane, tile):
    width = x.shape[1]
    west = pltpu.roll(x, 1, 1)
    first = west[:, :128]
    before = jnp.where(tile == 0, pltpu.roll(first, 2, 0), pltpu.roll(first, 1, 0))
    first = jnp.where(lane == 0, before, first)
    west = jnp.concatenate([first, west[:, 128:]], axis=1)
    east = pltpu.roll(x, width - 1, 1)
    last = east[:, width - 128 :]
    after = jnp.where(tile == TILES_DEV - 1, pltpu.roll(last, 6, 0), pltpu.roll(last, 7, 0))
    last = jnp.where(lane == 127, after, last)
    east = jnp.concatenate([east[:, : width - 128], last], axis=1)
    return west, east


def kernel(
    outer_n, slots, splits,
    steps, prints, hot, hot2, flux, coef, sel, sel2, group, weights, weights2,
    out,
    send, arr, send2, arr2, halo_f, halo_c, field_a, field_b, cof, tiles, acc, val, ret, val2, ret2,
    f_send, f_recv, g_send, g_recv, h_send, h_recv, r_send, r_recv, l_send, l_recv, v_send, v_recv, w_send, w_recv,
):
    rows = flux.shape[0]
    wide = flux.shape[1]
    samples = wide // LANES_T
    count = outer_n * INNER
    me = lax.axis_index("station")
    outer, inner = me // INNER, lax.rem(me, INNER)
    base = outer * INNER
    has_up, has_down = me > 0, me < count - 1
    has_left, has_right = outer > 0, outer < outer_n - 1
    first, last = outer == 0, outer == outer_n - 1
    is_end = jnp.logical_or(first, last)
    is_next = jnp.logical_or(outer == 1, outer == outer_n - 2)
    other_base = jnp.where(first, 1, jnp.where(last, outer_n - 2, jnp.where(outer == 1, 0, outer_n - 1))) * INNER
    lone_left = jnp.logical_and(outer >= 2, outer <= outer_n - 2)
    lone_right = jnp.logical_and(outer >= 1, outer <= outer_n - 3)
    lone_up = jnp.logical_and(lone_left, inner == 0)
    lone_down = jnp.logical_and(lone_right, inner == INNER - 1)

    def peer(offset):
        return base + lax.rem(inner + offset, INNER)

    def across(offset):
        return other_base + lax.rem(inner + offset, INNER)

    barrier = pltpu.get_barrier_semaphore()

    def greet(device):
        pl.semaphore_signal(barrier, inc=1, device_id={"station": device}, device_id_type=MESH)

    for offset in range(1, INNER):
        greet(peer(offset))
    others = ((lone_left, -INNER), (lone_right, INNER), (lone_up, -1), (lone_down, 1))
    for there, step in others:
        @pl.when(there)
        def _():
            greet(me + step)

    paired = jnp.logical_or(is_end, is_next)

    @pl.when(paired)
    def _():
        for offset in range(INNER):
            greet(across(offset))
    pl.semaphore_wait(
        barrier,
        INNER - 1 + sum(jnp.where(there, 1, 0) for there, _ in others) + jnp.where(paired, INNER, 0),
    )

    def remote(src, dst, ssem, rsem, device):
        return pltpu.make_async_remote_copy(
            src_ref=src, dst_ref=dst, send_sem=ssem, recv_sem=rsem,
            device_id={"station": device}, device_id_type=MESH,
        )

    def halo_copies(way):
        step = -1 if way == 0 else 1
        cut = pl.ds(0, ITERS) if way == 0 else pl.ds(rows - ITERS, ITERS)
        return (
            remote(flux.at[cut], halo_f.at[1 - way], h_send.at[way, 0], h_recv.at[1 - way, 0], me + step),
            remote(coef.at[cut], halo_c.at[1 - way], h_send.at[way, 1], h_recv.at[1 - way, 1], me + step),
        )

    for way, there in ((0, has_up), (1, has_down)):
        @pl.when(there)
        def _():
            for copy in halo_copies(way):
                copy.start()

        @pl.when(jnp.logical_not(there))
        def _():
            halo_f[way] = jnp.zeros(halo_f.shape[1:], halo_f.dtype)
            halo_c[way] = jnp.zeros(halo_c.shape[1:], halo_c.dtype)

    cells = prints.shape[2]
    short = cells // splits

    def some_prints(at):
        block = prints[:, :, pl.ds(pl.multiple_of(at, 256), 256)]
        return block.reshape(block.shape[0] * KT, 256)

    own2 = pl.ds(pl.multiple_of(inner * GROUP_ROWS, GROUP_ROWS), GROUP_ROWS)

    def rows2(offset):
        return pl.ds(pl.multiple_of(lax.rem(inner + offset, INNER) * GROUP_ROWS, GROUP_ROWS), GROUP_ROWS)

    def group_copy(offset):
        return remote(send2.at[rows2(offset)], arr2.at[own2], g_send.at[offset], g_recv.at[offset], across(offset))

    @pl.when(is_end)
    def _():
        def pack2(i, carry):
            for j in range(2):
                at = i * 512 + j * 256
                stack = [some_prints(q * short + at) for q in range(splits)]
                packed = jnp.dot(hot2[...], jnp.concatenate(stack, axis=0), preferred_element_type=jnp.float32)
                send2[:, pl.ds(pl.multiple_of(at, 256), 256)] = packed.astype(jnp.bfloat16)
            return carry

        lax.fori_loop(0, short // 512, pack2, 0)
        for offset in range(INNER):
            group_copy(offset).start()
        missing = jnp.where(first, 1, outer_n - 2)

        def clear(r, carry):
            tiles[r, pl.ds(pl.multiple_of(missing * wide, wide), wide), :] = jnp.zeros((wide, TILE_LON), jnp.bfloat16)
            return carry

        lax.fori_loop(0, rows, clear, 0)

    length = cells // PIECES

    def print_copy(offset, c):
        target = peer(offset)
        lanes = pl.ds(pl.multiple_of(c * length, length), length)
        to_rows = pl.ds(pl.multiple_of(lax.rem(inner + offset, INNER) * slots, slots), slots)
        my_rows = pl.ds(pl.multiple_of(inner * slots, slots), slots)
        return remote(send.at[to_rows, lanes], arr.at[my_rows, lanes], f_send.at[offset, c], f_recv.at[offset, c], target)

    own = pl.ds(pl.multiple_of(inner * slots, slots), slots)

    def send_prints(c):
        for j in range(length // 256):
            at = c * length + j * 256
            packed = jnp.dot(hot[...], some_prints(at), preferred_element_type=jnp.float32)
            send[:, pl.ds(pl.multiple_of(at, 256), 256)] = packed.astype(jnp.bfloat16)
        for offset in range(1, INNER):
            print_copy(offset, c).start()

    for c in range(AHEAD):
        send_prints(c)

    def load(r, carry):
        field_a[r + ITERS] = flux[r].astype(jnp.float32)
        cof[r + ITERS] = coef[r]
        return carry

    lax.fori_loop(0, rows, load, 0)
    for way, there in ((0, has_up), (1, has_down)):
        @pl.when(there)
        def _():
            for copy in halo_copies(way):
                copy.wait_send()
            remote(flux.at[pl.ds(0, ITERS)], halo_f.at[way], h_send.at[way, 0], h_recv.at[way, 0], me).wait_recv()
            remote(coef.at[pl.ds(0, ITERS)], halo_c.at[way], h_send.at[way, 1], h_recv.at[way, 1], me).wait_recv()

    def load_halo(r, carry):
        field_a[r] = halo_f[0, r].astype(jnp.float32)
        cof[r] = halo_c[0, r]
        field_a[r + ITERS + rows] = halo_f[1, r].astype(jnp.float32)
        cof[r + ITERS + rows] = halo_c[1, r]
        return carry

    lax.fori_loop(0, ITERS, load_halo, 0)

    lane = lax.broadcasted_iota(jnp.int32, (LANES_T, 128), 1)
    tile = lax.broadcasted_iota(jnp.int32, (LANES_T, 128), 0)

    def updated(src, r, k, s):
        cut = slice(s * LANES_T, (s + 1) * LANES_T)
        center = src[r, cut, :]
        west, east = east_west(center, lane, tile)
        lap = src[r - 1, cut, :] + src[r + 1, cut, :] + west + east - 4.0 * center
        return center + jnp.where(k < steps[s], 1.0, 0.0) * cof[r] * lap

    piece = rows // PIECES

    def block_copy(block, c, k, to_right):
        at = tiles.at[pl.ds(c * piece, piece), pl.ds(pl.multiple_of(block * wide, wide), wide), :]
        if to_right:
            return remote(at, at, r_send.at[k, c], r_recv.at[k, c], me + INNER)
        return remote(at, at, l_send.at[k, c], l_recv.at[k, c], me - INNER)

    def goes(there, k, to_right):
        there = jnp.logical_and(there, has_right if to_right else has_left)
        if k == 0:
            there = jnp.logical_and(there, outer != (outer_n - 2 if to_right else 1))
        return there

    def start_block(block, c, k, to_right, there):
        @pl.when(goes(there, k, to_right))
        def _():
            block_copy(block, c, k, to_right).start()

    mine = pl.ds(pl.multiple_of(outer * wide, wide), wide)

    def step_row(r, k):
        src, dst = (field_a, field_b) if k % 2 == 0 else (field_b, field_a)
        done = [updated(src, r, k, s) for s in range(samples)]
        if k == ITERS - 1:
            tiles[r - ITERS, mine, :] = jnp.concatenate(done, axis=0).astype(jnp.bfloat16)
        else:
            for s in range(samples):
                dst[r, s * LANES_T : (s + 1) * LANES_T, :] = done[s]

    def send_piece(c):
        start_block(outer, c, 0, True, has_right)
        start_block(outer, c, 0, False, has_left)

    for k in range(ITERS):
        def row_pair(i, carry, k=k):
            step_row(k + 1 + 2 * i, k)
            step_row(k + 2 + 2 * i, k)
            return carry

        lax.fori_loop(0, piece // 2 + ITERS - 1 - k, row_pair, 0)
    send_piece(0)

    def reach(k):
        from_left, from_right = outer - 1 - k >= 0, outer + 1 + k < outer_n
        if k == 0:
            from_left = jnp.logical_and(from_left, jnp.logical_not(last))
            from_right = jnp.logical_and(from_right, jnp.logical_not(first))
        return from_left, from_right

    def relay(c, k):
        from_left, from_right = reach(k)

        @pl.when(from_left)
        def _():
            block_copy(outer - 1 - k, c, k, True).wait_recv()

        if k < outer_n - 2:
            start_block(outer - 1 - k, c, k + 1, True, from_left)

        @pl.when(from_right)
        def _():
            block_copy(outer + 1 + k, c, k, False).wait_recv()

        if k < outer_n - 2:
            start_block(outer + 1 + k, c, k + 1, False, from_right)

    def next_piece(c):
        for k in range(ITERS):
            for j in range(piece):
                step_row(c * piece + 2 * ITERS - 1 - k + j, k)
        send_piece(c)
        relay(c - 1, 0)

    def piece_and_prints(c, carry):
        next_piece(c)
        send_prints(c + AHEAD - 1)
        return carry

    def piece_alone(c, carry):
        next_piece(c)
        return carry

    lax.fori_loop(1, PIECES + 1 - AHEAD, piece_and_prints, 0)
    lax.fori_loop(PIECES + 1 - AHEAD, PIECES, piece_alone, 0)
    arr[own, :] = send[own, :]

    def multiply(c):
        for offset in range(1, INNER):
            print_copy(offset, c).wait_recv()
        total = jnp.zeros(acc.shape, jnp.float32) if c == 0 else acc[...]
        for r in range(c * piece, (c + 1) * piece):
            total = total + lax.dot_general(
                arr[:, r * TILE_LON : (r + 1) * TILE_LON], tiles[r], (((1,), (1,)), ((), ())),
                preferred_element_type=jnp.float32,
            )
        acc[...] = total

    def value_copy2(offset):
        return remote(val2.at[rows2(offset)], ret2.at[own2], w_send.at[offset], w_recv.at[offset], across(offset))

    def group_values():
        for offset in range(INNER):
            group_copy(offset).wait_recv()
        per_split = rows // splits
        total = jnp.zeros(sel2.shape[1:], jnp.float32)
        for q in range(splits):
            def add_row(r, part, q=q):
                return part + lax.dot_general(
                    arr2[:, pl.ds(pl.multiple_of(r * TILE_LON, TILE_LON), TILE_LON)],
                    tiles[q * per_split + r, mine, :], (((1,), (1,)), ((), ())),
                    preferred_element_type=jnp.float32,
                )

            part = jnp.zeros(sel2.shape[1:], jnp.float32)
            for r in range(per_split):
                part = add_row(r, part)
            total = total + part * sel2[q]
        val2[...] = jnp.dot(total, group[:wide, :], precision=lax.Precision.HIGHEST, preferred_element_type=jnp.float32)
        for offset in range(INNER):
            value_copy2(offset).start()

    for k in range(outer_n - 1):
        for c in range(PIECES):
            if k > 0 or c == PIECES - 1:
                relay(c, k)

            if k >= outer_n - 3:
                @pl.when(is_end if k == outer_n - 2 else jnp.logical_not(is_end))
                def _():
                    multiply(c)

        if k == 0:
            pl.when(is_next)(group_values)

    val[...] = jnp.dot(acc[...] * sel[...], group[...], precision=lax.Precision.HIGHEST, preferred_element_type=jnp.float32)

    def value_copy(offset):
        to_rows = pl.ds(pl.multiple_of(lax.rem(inner + offset, INNER) * slots, slots), slots)
        return remote(val.at[to_rows], ret.at[own], v_send.at[offset], v_recv.at[offset], peer(offset))

    for offset in range(1, INNER):
        value_copy(offset).start()
    ret[own, :] = val[own, :]
    for offset in range(1, INNER):
        value_copy(offset).wait_recv()
    out[...] = jnp.dot(weights[...], ret[...], precision=lax.Precision.HIGHEST, preferred_element_type=jnp.float32)

    @pl.when(is_end)
    def _():
        for offset in range(INNER):
            value_copy2(offset).wait_recv()
        out[...] += jnp.dot(weights2[...], ret2[...], precision=lax.Precision.HIGHEST, preferred_element_type=jnp.float32)
        for offset in range(INNER):
            group_copy(offset).wait_send()

    @pl.when(is_next)
    def _():
        for offset in range(INNER):
            value_copy2(offset).wait_send()

    for offset in range(1, INNER):
        value_copy(offset).wait_send()
        for c in range(PIECES):
            print_copy(offset, c).wait_send()
    for k in range(outer_n - 1):
        for c in range(PIECES):
            @pl.when(goes(outer - k >= 0, k, True))
            def _():
                block_copy(outer - k, c, k, True).wait_send()

            @pl.when(goes(outer + k < outer_n, k, False))
            def _():
                block_copy(outer + k, c, k, False).wait_send()


def body(flux, coeff, diff_steps, footprint, tile_src, tile_local, tile_count):
    samples, rows, _ = flux.shape
    stations = footprint.shape[0]
    devices = lax.axis_size("station")
    outer_n = devices // INNER
    me = lax.axis_index("station")
    outer, inner = me // INNER, me % INNER
    slot_count = stations * KT
    cap = 2 * max(1, (slot_count + devices - 1) // devices)
    slots = outer_n * cap
    wide = samples * LANES_T

    flux_t = flux.reshape(samples, rows, TILES_DEV, TILE_LON).transpose(1, 0, 2, 3)
    flux_t = jnp.pad(flux_t, ((0, 0), (0, 0), (0, 1), (0, 0))).reshape(rows, wide, TILE_LON)
    coef_t = jnp.pad(coeff.reshape(rows, TILES_DEV, TILE_LON), ((0, 0), (0, 1), (0, 0)))

    order = jnp.arange(slot_count, dtype=jnp.int32)
    listed = (tile_src[:, :, 0] * LANES_T + tile_local).reshape(devices, slot_count)
    here = lax.dynamic_slice_in_dim(listed, outer * INNER, INNER, 0)
    src, loc = here // LANES_T, here % LANES_T
    target = src % INNER
    band_layer = src // INNER
    beside = jnp.where(outer == 0, 1, jnp.where(outer == outer_n - 1, outer_n - 2, -1))
    grouped = band_layer == beside
    target = jnp.where(grouped, INNER + target, target)
    same = (target[:, :, None] == target[:, None, :]) & (order[None, :] < order[:, None])[None]
    rank = jnp.sum(same.astype(jnp.int32), axis=2)
    places = jnp.arange(slots, dtype=jnp.int32)
    my_target = lax.dynamic_index_in_dim(target, inner, 0, keepdims=False)
    my_rank = lax.dynamic_index_in_dim(rank, inner, 0, keepdims=False)
    place = jnp.where(my_target < INNER, my_target * slots + my_rank, -1)
    hot = place[None, :] == jnp.arange(INNER * slots, dtype=jnp.int32)[:, None]
    splits = GROUP_ROWS // cap
    group_rows = jnp.arange(INNER * GROUP_ROWS, dtype=jnp.int32)
    row_owner, row_split, row_slot = group_rows // GROUP_ROWS, group_rows % GROUP_ROWS // cap, group_rows % cap
    in_group = (my_target[None, :] == INNER + row_owner[:, None]) & (my_rank[None, :] == row_slot[:, None])
    hot2 = in_group[:, None, :] & (row_split[:, None] == jnp.arange(splits, dtype=jnp.int32)[None, :])[:, :, None]
    hot2 = hot2.reshape(INNER * GROUP_ROWS, splits * slot_count)
    from_layer = jnp.where(outer == 1, 0, outer_n - 1)
    there = lax.dynamic_slice_in_dim(listed, from_layer * INNER, INNER, 0)
    src_end, loc_end = there // LANES_T, there % LANES_T
    to_me = src_end == me
    rank_end = jnp.sum((to_me[:, None, :] & (order[None, :] < order[:, None])[None]).astype(jnp.int32), axis=2)
    taken = to_me[:, None, :] & (rank_end[:, None, :] == jnp.arange(cap, dtype=jnp.int32)[None, :, None])
    tile_end = jnp.sum(jnp.where(taken, loc_end[:, None, :] + 1, 0), axis=2) - 1
    tile_end = jnp.broadcast_to(tile_end[:, None, :], (INNER, splits, cap)).reshape(INNER * GROUP_ROWS)
    sel2 = (tile_end[None, :, None] == (jnp.arange(wide, dtype=jnp.int32) % LANES_T)[None, None, :]) & (
        row_split[None, :, None] == jnp.arange(splits, dtype=jnp.int32)[:, None, None]
    )
    chosen = (target[:, None, :] == inner) & (rank[:, None, :] == places[None, :, None])
    code = band_layer * LANES_T + loc + 1
    named = jnp.sum(jnp.where(chosen, code[:, None, :], 0), axis=2).reshape(INNER * slots) - 1
    columns = jnp.arange(outer_n * wide, dtype=jnp.int32)
    column_code = (columns // wide) * LANES_T + columns % LANES_T
    sel = (named[:, None] == column_code[None, :]).astype(jnp.float32)
    group = ((columns % wide) // LANES_T)[:, None] == jnp.arange(128, dtype=jnp.int32)[None, :]
    live = (jnp.arange(KT, dtype=jnp.int32)[None, :] < tile_count[:, None]).reshape(slot_count)
    mine = (order // KT)[None, :] == jnp.arange(stations, dtype=jnp.int32)[:, None]
    hits = (mine & live[None, :])[:, :, None] & (place[None, :, None] == jnp.arange(INNER * slots, dtype=jnp.int32)[None, None, :])
    weights = jnp.sum(hits.astype(jnp.float32), axis=1)
    weights2 = jnp.sum(((mine & live[None, :])[:, None, :] & in_group[None]).astype(jnp.float32), axis=2)

    ext = rows + 2 * ITERS
    vmem = pl.BlockSpec(memory_space=pltpu.VMEM)
    dma = pltpu.SemaphoreType.DMA
    observed = pl.pallas_call(
        functools.partial(kernel, outer_n, slots, splits),
        out_shape=jax.ShapeDtypeStruct((stations, 128), jnp.float32),
        in_specs=[pl.BlockSpec(memory_space=pltpu.SMEM)] + [vmem] * 10,
        out_specs=vmem,
        scratch_shapes=[
            pltpu.VMEM((INNER * slots, footprint.shape[2]), jnp.bfloat16),
            pltpu.VMEM((INNER * slots, footprint.shape[2]), jnp.bfloat16),
            pltpu.VMEM((INNER * GROUP_ROWS, footprint.shape[2] // splits), jnp.bfloat16),
            pltpu.VMEM((INNER * GROUP_ROWS, footprint.shape[2] // splits), jnp.bfloat16),
            pltpu.VMEM((2, ITERS, wide, TILE_LON), jnp.bfloat16),
            pltpu.VMEM((2, ITERS, LANES_T, TILE_LON), jnp.float32),
            pltpu.VMEM((ext, wide, TILE_LON), jnp.float32),
            pltpu.VMEM((ext, wide, TILE_LON), jnp.float32),
            pltpu.VMEM((ext, LANES_T, TILE_LON), jnp.float32),
            pltpu.VMEM((rows, outer_n * wide, TILE_LON), jnp.bfloat16),
            pltpu.VMEM((INNER * slots, outer_n * wide), jnp.float32),
            pltpu.VMEM((INNER * slots, 128), jnp.float32),
            pltpu.VMEM((INNER * slots, 128), jnp.float32),
            pltpu.VMEM((INNER * GROUP_ROWS, 128), jnp.float32),
            pltpu.VMEM((INNER * GROUP_ROWS, 128), jnp.float32),
            dma((INNER, PIECES)), dma((INNER, PIECES)),
            dma((INNER,)), dma((INNER,)),
            dma((2, 2)), dma((2, 2)),
            dma((outer_n - 1, PIECES)), dma((outer_n - 1, PIECES)),
            dma((outer_n - 1, PIECES)), dma((outer_n - 1, PIECES)),
            dma((INNER,)), dma((INNER,)),
            dma((INNER,)), dma((INNER,)),
        ],
        compiler_params=pltpu.CompilerParams(
            collective_id=0, has_side_effects=True, vmem_limit_bytes=50 * 1024 * 1024
        ),
    )(
        diff_steps, footprint, hot.astype(jnp.bfloat16),
        hot2.astype(jnp.bfloat16), flux_t, coef_t, sel, sel2.astype(jnp.float32), group.astype(jnp.float32),
        weights, weights2,
    )
    return lax.all_gather(observed[:, :samples], "sample", axis=1, tiled=True)


def solution(mesh):
    in_specs = (
        P("sample", "station", None),
        P("station", None),
        P("sample"),
        P("station", None, None),
        P(),
        P(),
        P("station"),
    )
    out_specs = P("station", None)
    return jax.shard_map(body, mesh=mesh, in_specs=in_specs, out_specs=out_specs, check_vma=False)
```

```python
import functools

import jax
import jax.numpy as jnp
from jax import lax
from jax.experimental import pallas as pl
from jax.experimental.pallas import tpu as pltpu
from jax.sharding import PartitionSpec as P

TILE_LON = 512
TILES_DEV = 7
LANES_T = 8
KT = 4
ITERS = 6
INNER = 8
PIECES = 8
GROUP_ROWS = 16
MESH = pl.DeviceIdType.MESH


def east_west(x, lane, tile):
    width = x.shape[1]
    west = pltpu.roll(x, 1, 1)
    first = west[:, :128]
    before = jnp.where(tile == 0, pltpu.roll(first, 2, 0), pltpu.roll(first, 1, 0))
    first = jnp.where(lane == 0, before, first)
    west = jnp.concatenate([first, west[:, 128:]], axis=1)
    east = pltpu.roll(x, width - 1, 1)
    last = east[:, width - 128 :]
    after = jnp.where(tile == TILES_DEV - 1, pltpu.roll(last, 6, 0), pltpu.roll(last, 7, 0))
    last = jnp.where(lane == 127, after, last)
    east = jnp.concatenate([east[:, : width - 128], last], axis=1)
    return west, east


def kernel(
    outer_n, slots, splits,
    steps, prints, hot, hot2, flux, coef, sel, sel2, group, weights, weights2,
    out,
    send, arr, send2, arr2, halo_f, halo_c, field_a, field_b, cof, tiles, acc, val, ret, val2, ret2,
    f_send, f_recv, g_send, g_recv, h_send, h_recv, r_send, r_recv, l_send, l_recv, v_send, v_recv, w_send, w_recv,
):
    rows = flux.shape[0]
    wide = flux.shape[1]
    samples = wide // LANES_T
    count = outer_n * INNER
    me = lax.axis_index("station")
    outer, inner = me // INNER, lax.rem(me, INNER)
    base = outer * INNER
    has_up, has_down = me > 0, me < count - 1
    has_left, has_right = outer > 0, outer < outer_n - 1
    first, last = outer == 0, outer == outer_n - 1
    is_end = jnp.logical_or(first, last)
    is_next = jnp.logical_or(outer == 1, outer == outer_n - 2)
    other_base = jnp.where(first, 1, jnp.where(last, outer_n - 2, jnp.where(outer == 1, 0, outer_n - 1))) * INNER
    lone_left = jnp.logical_and(outer >= 2, outer <= outer_n - 2)
    lone_right = jnp.logical_and(outer >= 1, outer <= outer_n - 3)
    lone_up = jnp.logical_and(lone_left, inner == 0)
    lone_down = jnp.logical_and(lone_right, inner == INNER - 1)

    def peer(offset):
        return base + lax.rem(inner + offset, INNER)

    def across(offset):
        return other_base + lax.rem(inner + offset, INNER)

    barrier = pltpu.get_barrier_semaphore()

    def greet(device):
        pl.semaphore_signal(barrier, inc=1, device_id={"station": device}, device_id_type=MESH)

    for offset in range(1, INNER):
        greet(peer(offset))
    others = ((lone_left, -INNER), (lone_right, INNER), (lone_up, -1), (lone_down, 1))
    for there, step in others:
        @pl.when(there)
        def _():
            greet(me + step)

    paired = jnp.logical_or(is_end, is_next)

    @pl.when(paired)
    def _():
        for offset in range(INNER):
            greet(across(offset))
    pl.semaphore_wait(
        barrier,
        INNER - 1 + sum(jnp.where(there, 1, 0) for there, _ in others) + jnp.where(paired, INNER, 0),
    )

    def remote(src, dst, ssem, rsem, device):
        return pltpu.make_async_remote_copy(
            src_ref=src, dst_ref=dst, send_sem=ssem, recv_sem=rsem,
            device_id={"station": device}, device_id_type=MESH,
        )

    def halo_copies(way):
        step = -1 if way == 0 else 1
        cut = pl.ds(0, ITERS) if way == 0 else pl.ds(rows - ITERS, ITERS)
        return (
            remote(flux.at[cut], halo_f.at[1 - way], h_send.at[way, 0], h_recv.at[1 - way, 0], me + step),
            remote(coef.at[cut], halo_c.at[1 - way], h_send.at[way, 1], h_recv.at[1 - way, 1], me + step),
        )

    for way, there in ((0, has_up), (1, has_down)):
        @pl.when(there)
        def _():
            for copy in halo_copies(way):
                copy.start()

        @pl.when(jnp.logical_not(there))
        def _():
            halo_f[way] = jnp.zeros(halo_f.shape[1:], halo_f.dtype)
            halo_c[way] = jnp.zeros(halo_c.shape[1:], halo_c.dtype)

    cells = prints.shape[2]
    short = cells // splits

    def some_prints(at):
        block = prints[:, :, pl.ds(pl.multiple_of(at, 256), 256)]
        return block.reshape(block.shape[0] * KT, 256)

    own2 = pl.ds(pl.multiple_of(inner * GROUP_ROWS, GROUP_ROWS), GROUP_ROWS)

    def rows2(offset):
        return pl.ds(pl.multiple_of(lax.rem(inner + offset, INNER) * GROUP_ROWS, GROUP_ROWS), GROUP_ROWS)

    def group_copy(offset):
        return remote(send2.at[rows2(offset)], arr2.at[own2], g_send.at[offset], g_recv.at[offset], across(offset))

    @pl.when(is_end)
    def _():
        def pack2(i, carry):
            for j in range(2):
                at = i * 512 + j * 256
                stack = [some_prints(q * short + at) for q in range(splits)]
                packed = jnp.dot(hot2[...], jnp.concatenate(stack, axis=0), preferred_element_type=jnp.float32)
                send2[:, pl.ds(pl.multiple_of(at, 256), 256)] = packed.astype(jnp.bfloat16)
            return carry

        lax.fori_loop(0, short // 512, pack2, 0)
        for offset in range(INNER):
            group_copy(offset).start()
        missing = jnp.where(first, 1, outer_n - 2)

        def clear(r, carry):
            tiles[r, pl.ds(pl.multiple_of(missing * wide, wide), wide), :] = jnp.zeros((wide, TILE_LON), jnp.bfloat16)
            return carry

        lax.fori_loop(0, rows, clear, 0)

    length = cells // PIECES

    def print_copy(offset, c):
        target = peer(offset)
        lanes = pl.ds(pl.multiple_of(c * length, length), length)
        to_rows = pl.ds(pl.multiple_of(lax.rem(inner + offset, INNER) * slots, slots), slots)
        my_rows = pl.ds(pl.multiple_of(inner * slots, slots), slots)
        return remote(send.at[to_rows, lanes], arr.at[my_rows, lanes], f_send.at[offset, c], f_recv.at[offset, c], target)

    own = pl.ds(pl.multiple_of(inner * slots, slots), slots)

    def send_prints(c):
        for j in range(length // 256):
            at = c * length + j * 256
            packed = jnp.dot(hot[...], some_prints(at), preferred_element_type=jnp.float32)
            send[:, pl.ds(pl.multiple_of(at, 256), 256)] = packed.astype(jnp.bfloat16)
        for offset in range(1, INNER):
            print_copy(offset, c).start()

    def load(r, carry):
        field_a[r + ITERS] = flux[r].astype(jnp.float32)
        cof[r + ITERS] = coef[r]
        return carry

    lax.fori_loop(0, rows, load, 0)
    for way, there in ((0, has_up), (1, has_down)):
        @pl.when(there)
        def _():
            for copy in halo_copies(way):
                copy.wait_send()
            remote(flux.at[pl.ds(0, ITERS)], halo_f.at[way], h_send.at[way, 0], h_recv.at[way, 0], me).wait_recv()
            remote(coef.at[pl.ds(0, ITERS)], halo_c.at[way], h_send.at[way, 1], h_recv.at[way, 1], me).wait_recv()

    def load_halo(r, carry):
        field_a[r] = halo_f[0, r].astype(jnp.float32)
        cof[r] = halo_c[0, r]
        field_a[r + ITERS + rows] = halo_f[1, r].astype(jnp.float32)
        cof[r + ITERS + rows] = halo_c[1, r]
        return carry

    lax.fori_loop(0, ITERS, load_halo, 0)

    lane = lax.broadcasted_iota(jnp.int32, (LANES_T, 128), 1)
    tile = lax.broadcasted_iota(jnp.int32, (LANES_T, 128), 0)

    def updated(src, r, k, s):
        cut = slice(s * LANES_T, (s + 1) * LANES_T)
        center = src[r, cut, :]
        west, east = east_west(center, lane, tile)
        lap = src[r - 1, cut, :] + src[r + 1, cut, :] + west + east - 4.0 * center
        return center + jnp.where(k < steps[s], 1.0, 0.0) * cof[r] * lap

    piece = rows // PIECES

    def block_copy(block, c, k, to_right):
        at = tiles.at[pl.ds(c * piece, piece), pl.ds(pl.multiple_of(block * wide, wide), wide), :]
        if to_right:
            return remote(at, at, r_send.at[k, c], r_recv.at[k, c], me + INNER)
        return remote(at, at, l_send.at[k, c], l_recv.at[k, c], me - INNER)

    def goes(there, k, to_right):
        there = jnp.logical_and(there, has_right if to_right else has_left)
        if k == 0:
            there = jnp.logical_and(there, outer != (outer_n - 2 if to_right else 1))
        return there

    def start_block(block, c, k, to_right, there):
        @pl.when(goes(there, k, to_right))
        def _():
            block_copy(block, c, k, to_right).start()

    mine = pl.ds(pl.multiple_of(outer * wide, wide), wide)

    def step_row(r, k):
        src, dst = (field_a, field_b) if k % 2 == 0 else (field_b, field_a)
        done = [updated(src, r, k, s) for s in range(samples)]
        if k == ITERS - 1:
            tiles[r - ITERS, mine, :] = jnp.concatenate(done, axis=0).astype(jnp.bfloat16)
        else:
            for s in range(samples):
                dst[r, s * LANES_T : (s + 1) * LANES_T, :] = done[s]

    def send_piece(c):
        start_block(outer, c, 0, True, has_right)
        start_block(outer, c, 0, False, has_left)

    for k in range(ITERS):
        def row_pair(i, carry, k=k):
            step_row(k + 1 + 2 * i, k)
            step_row(k + 2 + 2 * i, k)
            return carry

        lax.fori_loop(0, piece // 2 + ITERS - 1 - k, row_pair, 0)
    send_piece(0)
    send_prints(0)

    def reach(k):
        from_left, from_right = outer - 1 - k >= 0, outer + 1 + k < outer_n
        if k == 0:
            from_left = jnp.logical_and(from_left, jnp.logical_not(last))
            from_right = jnp.logical_and(from_right, jnp.logical_not(first))
        return from_left, from_right

    def relay(c, k, begun=True):
        from_left, from_right = (jnp.logical_and(there, begun) for there in reach(k))

        @pl.when(from_left)
        def _():
            block_copy(outer - 1 - k, c, k, True).wait_recv()

        if k < outer_n - 2:
            start_block(outer - 1 - k, c, k + 1, True, from_left)

        @pl.when(from_right)
        def _():
            block_copy(outer + 1 + k, c, k, False).wait_recv()

        if k < outer_n - 2:
            start_block(outer + 1 + k, c, k + 1, False, from_right)

    def next_piece(c, carry):
        for k in range(ITERS):
            for j in range(piece):
                step_row(c * piece + 2 * ITERS - 1 - k + j, k)
        send_piece(c)
        relay(c - 1, 0)
        relay(c - 2, 1, c >= 2)
        send_prints(c)
        return carry

    lax.fori_loop(1, PIECES, next_piece, 0)
    relay(PIECES - 1, 0)
    relay(PIECES - 2, 1)
    relay(PIECES - 1, 1)
    arr[own, :] = send[own, :]

    def multiply(c):
        for offset in range(1, INNER):
            print_copy(offset, c).wait_recv()
        total = jnp.zeros(acc.shape, jnp.float32) if c == 0 else acc[...]
        for r in range(c * piece, (c + 1) * piece):
            total = total + lax.dot_general(
                arr[:, r * TILE_LON : (r + 1) * TILE_LON], tiles[r], (((1,), (1,)), ((), ())),
                preferred_element_type=jnp.float32,
            )
        acc[...] = total

    def value_copy2(offset):
        return remote(val2.at[rows2(offset)], ret2.at[own2], w_send.at[offset], w_recv.at[offset], across(offset))

    def group_values():
        for offset in range(INNER):
            group_copy(offset).wait_recv()
        per_split = rows // splits
        total = jnp.zeros(sel2.shape[1:], jnp.float32)
        for q in range(splits):
            def add_row(r, part, q=q):
                return part + lax.dot_general(
                    arr2[:, pl.ds(pl.multiple_of(r * TILE_LON, TILE_LON), TILE_LON)],
                    tiles[q * per_split + r, mine, :], (((1,), (1,)), ((), ())),
                    preferred_element_type=jnp.float32,
                )

            part = jnp.zeros(sel2.shape[1:], jnp.float32)
            for r in range(per_split):
                part = add_row(r, part)
            total = total + part * sel2[q]
        val2[...] = jnp.dot(total, group[:wide, :], precision=lax.Precision.HIGHEST, preferred_element_type=jnp.float32)
        for offset in range(INNER):
            value_copy2(offset).start()

    pl.when(is_next)(group_values)
    for k in range(2, outer_n - 1):
        for c in range(PIECES):
            relay(c, k)
            if k == outer_n - 2:
                multiply(c)

    val[...] = jnp.dot(acc[...] * sel[...], group[...], precision=lax.Precision.HIGHEST, preferred_element_type=jnp.float32)

    def value_copy(offset):
        to_rows = pl.ds(pl.multiple_of(lax.rem(inner + offset, INNER) * slots, slots), slots)
        return remote(val.at[to_rows], ret.at[own], v_send.at[offset], v_recv.at[offset], peer(offset))

    for offset in range(1, INNER):
        value_copy(offset).start()
    ret[own, :] = val[own, :]
    for offset in range(1, INNER):
        value_copy(offset).wait_recv()
    out[...] = jnp.dot(weights[...], ret[...], precision=lax.Precision.HIGHEST, preferred_element_type=jnp.float32)

    @pl.when(is_end)
    def _():
        for offset in range(INNER):
            value_copy2(offset).wait_recv()
        out[...] += jnp.dot(weights2[...], ret2[...], precision=lax.Precision.HIGHEST, preferred_element_type=jnp.float32)
        for offset in range(INNER):
            group_copy(offset).wait_send()

    @pl.when(is_next)
    def _():
        for offset in range(INNER):
            value_copy2(offset).wait_send()

    for offset in range(1, INNER):
        value_copy(offset).wait_send()
        for c in range(PIECES):
            print_copy(offset, c).wait_send()
    for k in range(outer_n - 1):
        for c in range(PIECES):
            @pl.when(goes(outer - k >= 0, k, True))
            def _():
                block_copy(outer - k, c, k, True).wait_send()

            @pl.when(goes(outer + k < outer_n, k, False))
            def _():
                block_copy(outer + k, c, k, False).wait_send()


def body(flux, coeff, diff_steps, footprint, tile_src, tile_local, tile_count):
    samples, rows, _ = flux.shape
    stations = footprint.shape[0]
    devices = lax.axis_size("station")
    outer_n = devices // INNER
    me = lax.axis_index("station")
    outer, inner = me // INNER, me % INNER
    slot_count = stations * KT
    cap = 2 * max(1, (slot_count + devices - 1) // devices)
    slots = outer_n * cap
    wide = samples * LANES_T

    flux_t = flux.reshape(samples, rows, TILES_DEV, TILE_LON).transpose(1, 0, 2, 3)
    flux_t = jnp.pad(flux_t, ((0, 0), (0, 0), (0, 1), (0, 0))).reshape(rows, wide, TILE_LON)
    coef_t = jnp.pad(coeff.reshape(rows, TILES_DEV, TILE_LON), ((0, 0), (0, 1), (0, 0)))

    order = jnp.arange(slot_count, dtype=jnp.int32)
    listed = (tile_src[:, :, 0] * LANES_T + tile_local).reshape(devices, slot_count)
    here = lax.dynamic_slice_in_dim(listed, outer * INNER, INNER, 0)
    src, loc = here // LANES_T, here % LANES_T
    target = src % INNER
    band_layer = src // INNER
    beside = jnp.where(outer == 0, 1, jnp.where(outer == outer_n - 1, outer_n - 2, -1))
    grouped = band_layer == beside
    target = jnp.where(grouped, INNER + target, target)
    same = (target[:, :, None] == target[:, None, :]) & (order[None, :] < order[:, None])[None]
    rank = jnp.sum(same.astype(jnp.int32), axis=2)
    places = jnp.arange(slots, dtype=jnp.int32)
    my_target = lax.dynamic_index_in_dim(target, inner, 0, keepdims=False)
    my_rank = lax.dynamic_index_in_dim(rank, inner, 0, keepdims=False)
    place = jnp.where(my_target < INNER, my_target * slots + my_rank, -1)
    hot = place[None, :] == jnp.arange(INNER * slots, dtype=jnp.int32)[:, None]
    splits = GROUP_ROWS // cap
    group_rows = jnp.arange(INNER * GROUP_ROWS, dtype=jnp.int32)
    row_owner, row_split, row_slot = group_rows // GROUP_ROWS, group_rows % GROUP_ROWS // cap, group_rows % cap
    in_group = (my_target[None, :] == INNER + row_owner[:, None]) & (my_rank[None, :] == row_slot[:, None])
    hot2 = in_group[:, None, :] & (row_split[:, None] == jnp.arange(splits, dtype=jnp.int32)[None, :])[:, :, None]
    hot2 = hot2.reshape(INNER * GROUP_ROWS, splits * slot_count)
    from_layer = jnp.where(outer == 1, 0, outer_n - 1)
    there = lax.dynamic_slice_in_dim(listed, from_layer * INNER, INNER, 0)
    src_end, loc_end = there // LANES_T, there % LANES_T
    to_me = src_end == me
    rank_end = jnp.sum((to_me[:, None, :] & (order[None, :] < order[:, None])[None]).astype(jnp.int32), axis=2)
    taken = to_me[:, None, :] & (rank_end[:, None, :] == jnp.arange(cap, dtype=jnp.int32)[None, :, None])
    tile_end = jnp.sum(jnp.where(taken, loc_end[:, None, :] + 1, 0), axis=2) - 1
    tile_end = jnp.broadcast_to(tile_end[:, None, :], (INNER, splits, cap)).reshape(INNER * GROUP_ROWS)
    sel2 = (tile_end[None, :, None] == (jnp.arange(wide, dtype=jnp.int32) % LANES_T)[None, None, :]) & (
        row_split[None, :, None] == jnp.arange(splits, dtype=jnp.int32)[:, None, None]
    )
    chosen = (target[:, None, :] == inner) & (rank[:, None, :] == places[None, :, None])
    code = band_layer * LANES_T + loc + 1
    named = jnp.sum(jnp.where(chosen, code[:, None, :], 0), axis=2).reshape(INNER * slots) - 1
    columns = jnp.arange(outer_n * wide, dtype=jnp.int32)
    column_code = (columns // wide) * LANES_T + columns % LANES_T
    sel = (named[:, None] == column_code[None, :]).astype(jnp.float32)
    group = ((columns % wide) // LANES_T)[:, None] == jnp.arange(128, dtype=jnp.int32)[None, :]
    live = (jnp.arange(KT, dtype=jnp.int32)[None, :] < tile_count[:, None]).reshape(slot_count)
    mine = (order // KT)[None, :] == jnp.arange(stations, dtype=jnp.int32)[:, None]
    hits = (mine & live[None, :])[:, :, None] & (place[None, :, None] == jnp.arange(INNER * slots, dtype=jnp.int32)[None, None, :])
    weights = jnp.sum(hits.astype(jnp.float32), axis=1)
    weights2 = jnp.sum(((mine & live[None, :])[:, None, :] & in_group[None]).astype(jnp.float32), axis=2)

    ext = rows + 2 * ITERS
    vmem = pl.BlockSpec(memory_space=pltpu.VMEM)
    dma = pltpu.SemaphoreType.DMA
    observed = pl.pallas_call(
        functools.partial(kernel, outer_n, slots, splits),
        out_shape=jax.ShapeDtypeStruct((stations, 128), jnp.float32),
        in_specs=[pl.BlockSpec(memory_space=pltpu.SMEM)] + [vmem] * 10,
        out_specs=vmem,
        scratch_shapes=[
            pltpu.VMEM((INNER * slots, footprint.shape[2]), jnp.bfloat16),
            pltpu.VMEM((INNER * slots, footprint.shape[2]), jnp.bfloat16),
            pltpu.VMEM((INNER * GROUP_ROWS, footprint.shape[2] // splits), jnp.bfloat16),
            pltpu.VMEM((INNER * GROUP_ROWS, footprint.shape[2] // splits), jnp.bfloat16),
            pltpu.VMEM((2, ITERS, wide, TILE_LON), jnp.bfloat16),
            pltpu.VMEM((2, ITERS, LANES_T, TILE_LON), jnp.float32),
            pltpu.VMEM((ext, wide, TILE_LON), jnp.float32),
            pltpu.VMEM((ext, wide, TILE_LON), jnp.float32),
            pltpu.VMEM((ext, LANES_T, TILE_LON), jnp.float32),
            pltpu.VMEM((rows, outer_n * wide, TILE_LON), jnp.bfloat16),
            pltpu.VMEM((INNER * slots, outer_n * wide), jnp.float32),
            pltpu.VMEM((INNER * slots, 128), jnp.float32),
            pltpu.VMEM((INNER * slots, 128), jnp.float32),
            pltpu.VMEM((INNER * GROUP_ROWS, 128), jnp.float32),
            pltpu.VMEM((INNER * GROUP_ROWS, 128), jnp.float32),
            dma((INNER, PIECES)), dma((INNER, PIECES)),
            dma((INNER,)), dma((INNER,)),
            dma((2, 2)), dma((2, 2)),
            dma((outer_n - 1, PIECES)), dma((outer_n - 1, PIECES)),
            dma((outer_n - 1, PIECES)), dma((outer_n - 1, PIECES)),
            dma((INNER,)), dma((INNER,)),
            dma((INNER,)), dma((INNER,)),
        ],
        compiler_params=pltpu.CompilerParams(
            collective_id=0, has_side_effects=True, vmem_limit_bytes=50 * 1024 * 1024
        ),
    )(
        diff_steps, footprint, hot.astype(jnp.bfloat16),
        hot2.astype(jnp.bfloat16), flux_t, coef_t, sel, sel2.astype(jnp.float32), group.astype(jnp.float32),
        weights, weights2,
    )
    return lax.all_gather(observed[:, :samples], "sample", axis=1, tiled=True)


def solution(mesh):
    in_specs = (
        P("sample", "station", None),
        P("station", None),
        P("sample"),
        P("station", None, None),
        P(),
        P(),
        P("station"),
    )
    out_specs = P("station", None)
    return jax.shard_map(body, mesh=mesh, in_specs=in_specs, out_specs=out_specs, check_vma=False)
```

```python
import functools

import jax
import jax.numpy as jnp
from jax import lax
from jax.experimental import pallas as pl
from jax.experimental.pallas import tpu as pltpu
from jax.sharding import PartitionSpec as P

TILE_LON = 512
TILES_DEV = 7
LANES_T = 8
KT = 4
ITERS = 6
INNER = 8
PIECES = 8
GROUP_ROWS = 16
MESH = pl.DeviceIdType.MESH


def east_west(x, lane, tile):
    width = x.shape[1]
    west = pltpu.roll(x, 1, 1)
    first = west[:, :128]
    before = jnp.where(tile == 0, pltpu.roll(first, 2, 0), pltpu.roll(first, 1, 0))
    first = jnp.where(lane == 0, before, first)
    west = jnp.concatenate([first, west[:, 128:]], axis=1)
    east = pltpu.roll(x, width - 1, 1)
    last = east[:, width - 128 :]
    after = jnp.where(tile == TILES_DEV - 1, pltpu.roll(last, 6, 0), pltpu.roll(last, 7, 0))
    last = jnp.where(lane == 127, after, last)
    east = jnp.concatenate([east[:, : width - 128], last], axis=1)
    return west, east


def kernel(
    outer_n, slots, splits,
    steps, prints, hot, hot2, flux, coef, sel, sel2, group, weights, weights2,
    out,
    send, arr, send2, arr2, halo_f, halo_c, field_a, field_b, cof, tiles, acc, val, ret, val2, ret2,
    f_send, f_recv, g_send, g_recv, h_send, h_recv, r_send, r_recv, l_send, l_recv, v_send, v_recv, w_send, w_recv,
):
    rows = flux.shape[0]
    wide = flux.shape[1]
    samples = wide // LANES_T
    count = outer_n * INNER
    me = lax.axis_index("station")
    outer, inner = me // INNER, lax.rem(me, INNER)
    base = outer * INNER
    has_up, has_down = me > 0, me < count - 1
    has_left, has_right = outer > 0, outer < outer_n - 1
    first, last = outer == 0, outer == outer_n - 1
    is_end = jnp.logical_or(first, last)
    is_next = jnp.logical_or(outer == 1, outer == outer_n - 2)
    other_base = jnp.where(first, 1, jnp.where(last, outer_n - 2, jnp.where(outer == 1, 0, outer_n - 1))) * INNER
    lone_left = jnp.logical_and(outer >= 2, outer <= outer_n - 2)
    lone_right = jnp.logical_and(outer >= 1, outer <= outer_n - 3)
    lone_up = jnp.logical_and(lone_left, inner == 0)
    lone_down = jnp.logical_and(lone_right, inner == INNER - 1)

    def peer(offset):
        return base + lax.rem(inner + offset, INNER)

    def across(offset):
        return other_base + lax.rem(inner + offset, INNER)

    barrier = pltpu.get_barrier_semaphore()

    def greet(device):
        pl.semaphore_signal(barrier, inc=1, device_id={"station": device}, device_id_type=MESH)

    for offset in range(1, INNER):
        greet(peer(offset))
    others = (
        (lone_left, -INNER), (lone_right, INNER), (lone_up, -1), (lone_down, 1),
        (first, 2 * INNER), (last, -2 * INNER), (outer == 2, -2 * INNER), (outer == outer_n - 3, 2 * INNER),
    )
    for there, step in others:
        @pl.when(there)
        def _():
            greet(me + step)

    paired = jnp.logical_or(is_end, is_next)

    @pl.when(paired)
    def _():
        for offset in range(INNER):
            greet(across(offset))
    pl.semaphore_wait(
        barrier,
        INNER - 1 + sum(jnp.where(there, 1, 0) for there, _ in others) + jnp.where(paired, INNER, 0),
    )

    def remote(src, dst, ssem, rsem, device):
        return pltpu.make_async_remote_copy(
            src_ref=src, dst_ref=dst, send_sem=ssem, recv_sem=rsem,
            device_id={"station": device}, device_id_type=MESH,
        )

    def halo_copies(way):
        step = -1 if way == 0 else 1
        cut = pl.ds(0, ITERS) if way == 0 else pl.ds(rows - ITERS, ITERS)
        return (
            remote(flux.at[cut], halo_f.at[1 - way], h_send.at[way, 0], h_recv.at[1 - way, 0], me + step),
            remote(coef.at[cut], halo_c.at[1 - way], h_send.at[way, 1], h_recv.at[1 - way, 1], me + step),
        )

    for way, there in ((0, has_up), (1, has_down)):
        @pl.when(there)
        def _():
            for copy in halo_copies(way):
                copy.start()

        @pl.when(jnp.logical_not(there))
        def _():
            halo_f[way] = jnp.zeros(halo_f.shape[1:], halo_f.dtype)
            halo_c[way] = jnp.zeros(halo_c.shape[1:], halo_c.dtype)

    cells = prints.shape[2]
    short = cells // splits

    def some_prints(at):
        block = prints[:, :, pl.ds(pl.multiple_of(at, 256), 256)]
        return block.reshape(block.shape[0] * KT, 256)

    own2 = pl.ds(pl.multiple_of(inner * GROUP_ROWS, GROUP_ROWS), GROUP_ROWS)

    def rows2(offset):
        return pl.ds(pl.multiple_of(lax.rem(inner + offset, INNER) * GROUP_ROWS, GROUP_ROWS), GROUP_ROWS)

    def group_copy(offset):
        return remote(send2.at[rows2(offset)], arr2.at[own2], g_send.at[offset], g_recv.at[offset], across(offset))

    @pl.when(is_end)
    def _():
        def pack2(i, carry):
            for j in range(2):
                at = i * 512 + j * 256
                stack = [some_prints(q * short + at) for q in range(splits)]
                packed = jnp.dot(hot2[...], jnp.concatenate(stack, axis=0), preferred_element_type=jnp.float32)
                send2[:, pl.ds(pl.multiple_of(at, 256), 256)] = packed.astype(jnp.bfloat16)
            return carry

        lax.fori_loop(0, short // 512, pack2, 0)
        for offset in range(INNER):
            group_copy(offset).start()
        missing = jnp.where(first, 1, outer_n - 2)

        def clear(r, carry):
            tiles[r, pl.ds(pl.multiple_of(missing * wide, wide), wide), :] = jnp.zeros((wide, TILE_LON), jnp.bfloat16)
            return carry

        lax.fori_loop(0, rows, clear, 0)

    length = cells // PIECES

    def print_copy(offset, c):
        target = peer(offset)
        lanes = pl.ds(pl.multiple_of(c * length, length), length)
        to_rows = pl.ds(pl.multiple_of(lax.rem(inner + offset, INNER) * slots, slots), slots)
        my_rows = pl.ds(pl.multiple_of(inner * slots, slots), slots)
        return remote(send.at[to_rows, lanes], arr.at[my_rows, lanes], f_send.at[offset, c], f_recv.at[offset, c], target)

    own = pl.ds(pl.multiple_of(inner * slots, slots), slots)

    def send_prints(c):
        for j in range(length // 256):
            at = c * length + j * 256
            packed = jnp.dot(hot[...], some_prints(at), preferred_element_type=jnp.float32)
            send[:, pl.ds(pl.multiple_of(at, 256), 256)] = packed.astype(jnp.bfloat16)
        for offset in range(1, INNER):
            print_copy(offset, c).start()

    def load(r, carry):
        field_a[r + ITERS] = flux[r].astype(jnp.float32)
        cof[r + ITERS] = coef[r]
        return carry

    lax.fori_loop(0, rows, load, 0)
    for way, there in ((0, has_up), (1, has_down)):
        @pl.when(there)
        def _():
            for copy in halo_copies(way):
                copy.wait_send()
            remote(flux.at[pl.ds(0, ITERS)], halo_f.at[way], h_send.at[way, 0], h_recv.at[way, 0], me).wait_recv()
            remote(coef.at[pl.ds(0, ITERS)], halo_c.at[way], h_send.at[way, 1], h_recv.at[way, 1], me).wait_recv()

    def load_halo(r, carry):
        field_a[r] = halo_f[0, r].astype(jnp.float32)
        cof[r] = halo_c[0, r]
        field_a[r + ITERS + rows] = halo_f[1, r].astype(jnp.float32)
        cof[r + ITERS + rows] = halo_c[1, r]
        return carry

    lax.fori_loop(0, ITERS, load_halo, 0)

    lane = lax.broadcasted_iota(jnp.int32, (LANES_T, 128), 1)
    tile = lax.broadcasted_iota(jnp.int32, (LANES_T, 128), 0)

    def updated(src, r, k, s):
        cut = slice(s * LANES_T, (s + 1) * LANES_T)
        center = src[r, cut, :]
        west, east = east_west(center, lane, tile)
        lap = src[r - 1, cut, :] + src[r + 1, cut, :] + west + east - 4.0 * center
        return center + jnp.where(k < steps[s], 1.0, 0.0) * cof[r] * lap

    piece = rows // PIECES

    def block_copy(block, c, k, to_right, hops=1):
        at = tiles.at[pl.ds(c * piece, piece), pl.ds(pl.multiple_of(block * wide, wide), wide), :]
        if to_right:
            return remote(at, at, r_send.at[k, c], r_recv.at[k, c], me + hops * INNER)
        return remote(at, at, l_send.at[k, c], l_recv.at[k, c], me - hops * INNER)

    def goes(there, k, to_right):
        there = jnp.logical_and(there, has_right if to_right else has_left)
        if k == 0:
            there = jnp.logical_and(there, outer != (outer_n - 2 if to_right else 1))
        if k == 1:
            there = jnp.logical_and(there, outer != (1 if to_right else outer_n - 2))
        return there

    def start_block(block, c, k, to_right, there):
        @pl.when(goes(there, k, to_right))
        def _():
            block_copy(block, c, k, to_right).start()

    mine = pl.ds(pl.multiple_of(outer * wide, wide), wide)

    def step_row(r, k):
        src, dst = (field_a, field_b) if k % 2 == 0 else (field_b, field_a)
        done = [updated(src, r, k, s) for s in range(samples)]
        if k == ITERS - 1:
            tiles[r - ITERS, mine, :] = jnp.concatenate(done, axis=0).astype(jnp.bfloat16)
        else:
            for s in range(samples):
                dst[r, s * LANES_T : (s + 1) * LANES_T, :] = done[s]

    def send_piece(c):
        start_block(outer, c, 0, True, has_right)
        start_block(outer, c, 0, False, has_left)
        for at_end, to_right in ((first, True), (last, False)):
            @pl.when(at_end)
            def _():
                block_copy(outer, c, 1, to_right, 2).start()

    for k in range(ITERS):
        def row_pair(i, carry, k=k):
            step_row(k + 1 + 2 * i, k)
            step_row(k + 2 + 2 * i, k)
            return carry

        lax.fori_loop(0, piece // 2 + ITERS - 1 - k, row_pair, 0)
    send_piece(0)
    send_prints(0)

    def reach(k):
        from_left, from_right = outer - 1 - k >= 0, outer + 1 + k < outer_n
        if k == 0:
            from_left = jnp.logical_and(from_left, jnp.logical_not(last))
            from_right = jnp.logical_and(from_right, jnp.logical_not(first))
        return from_left, from_right

    def relay(c, k, begun=True):
        from_left, from_right = (jnp.logical_and(there, begun) for there in reach(k))

        @pl.when(from_left)
        def _():
            block_copy(outer - 1 - k, c, k, True).wait_recv()

        if k < outer_n - 2:
            start_block(outer - 1 - k, c, k + 1, True, from_left)

        @pl.when(from_right)
        def _():
            block_copy(outer + 1 + k, c, k, False).wait_recv()

        if k < outer_n - 2:
            start_block(outer + 1 + k, c, k + 1, False, from_right)

    def next_piece(c, carry):
        for k in range(ITERS):
            for j in range(piece):
                step_row(c * piece + 2 * ITERS - 1 - k + j, k)
        send_piece(c)
        relay(c - 1, 0)
        relay(c - 2, 1, c >= 2)
        send_prints(c)
        return carry

    lax.fori_loop(1, PIECES, next_piece, 0)
    relay(PIECES - 1, 0)
    relay(PIECES - 2, 1)
    relay(PIECES - 1, 1)
    arr[own, :] = send[own, :]

    def multiply(c):
        for offset in range(1, INNER):
            print_copy(offset, c).wait_recv()
        total = jnp.zeros(acc.shape, jnp.float32) if c == 0 else acc[...]
        for r in range(c * piece, (c + 1) * piece):
            total = total + lax.dot_general(
                arr[:, r * TILE_LON : (r + 1) * TILE_LON], tiles[r], (((1,), (1,)), ((), ())),
                preferred_element_type=jnp.float32,
            )
        acc[...] = total

    def value_copy2(offset):
        return remote(val2.at[rows2(offset)], ret2.at[own2], w_send.at[offset], w_recv.at[offset], across(offset))

    def group_values():
        for offset in range(INNER):
            group_copy(offset).wait_recv()
        per_split = rows // splits
        total = jnp.zeros(sel2.shape[1:], jnp.float32)
        for q in range(splits):
            def add_row(r, part, q=q):
                return part + lax.dot_general(
                    arr2[:, pl.ds(pl.multiple_of(r * TILE_LON, TILE_LON), TILE_LON)],
                    tiles[q * per_split + r, mine, :], (((1,), (1,)), ((), ())),
                    preferred_element_type=jnp.float32,
                )

            part = jnp.zeros(sel2.shape[1:], jnp.float32)
            for r in range(per_split):
                part = add_row(r, part)
            total = total + part * sel2[q]
        val2[...] = jnp.dot(total, group[:wide, :], precision=lax.Precision.HIGHEST, preferred_element_type=jnp.float32)
        for offset in range(INNER):
            value_copy2(offset).start()

    pl.when(is_next)(group_values)
    for k in range(2, outer_n - 1):
        for c in range(PIECES):
            relay(c, k)
            if k == outer_n - 2:
                multiply(c)

    val[...] = jnp.dot(acc[...] * sel[...], group[...], precision=lax.Precision.HIGHEST, preferred_element_type=jnp.float32)

    def value_copy(offset):
        to_rows = pl.ds(pl.multiple_of(lax.rem(inner + offset, INNER) * slots, slots), slots)
        return remote(val.at[to_rows], ret.at[own], v_send.at[offset], v_recv.at[offset], peer(offset))

    for offset in range(1, INNER):
        value_copy(offset).start()
    ret[own, :] = val[own, :]
    for offset in range(1, INNER):
        value_copy(offset).wait_recv()
    out[...] = jnp.dot(weights[...], ret[...], precision=lax.Precision.HIGHEST, preferred_element_type=jnp.float32)

    @pl.when(is_end)
    def _():
        for offset in range(INNER):
            value_copy2(offset).wait_recv()
        out[...] += jnp.dot(weights2[...], ret2[...], precision=lax.Precision.HIGHEST, preferred_element_type=jnp.float32)
        for offset in range(INNER):
            group_copy(offset).wait_send()

    for at_end, to_right in ((first, True), (last, False)):
        @pl.when(at_end)
        def _():
            for c in range(PIECES):
                block_copy(outer, c, 1, to_right, 2).wait_send()

    @pl.when(is_next)
    def _():
        for offset in range(INNER):
            value_copy2(offset).wait_send()

    for offset in range(1, INNER):
        value_copy(offset).wait_send()
        for c in range(PIECES):
            print_copy(offset, c).wait_send()
    for k in range(outer_n - 1):
        for c in range(PIECES):
            @pl.when(goes(outer - k >= 0, k, True))
            def _():
                block_copy(outer - k, c, k, True).wait_send()

            @pl.when(goes(outer + k < outer_n, k, False))
            def _():
                block_copy(outer + k, c, k, False).wait_send()


def body(flux, coeff, diff_steps, footprint, tile_src, tile_local, tile_count):
    samples, rows, _ = flux.shape
    stations = footprint.shape[0]
    devices = lax.axis_size("station")
    outer_n = devices // INNER
    me = lax.axis_index("station")
    outer, inner = me // INNER, me % INNER
    slot_count = stations * KT
    cap = 2 * max(1, (slot_count + devices - 1) // devices)
    slots = outer_n * cap
    wide = samples * LANES_T

    flux_t = flux.reshape(samples, rows, TILES_DEV, TILE_LON).transpose(1, 0, 2, 3)
    flux_t = jnp.pad(flux_t, ((0, 0), (0, 0), (0, 1), (0, 0))).reshape(rows, wide, TILE_LON)
    coef_t = jnp.pad(coeff.reshape(rows, TILES_DEV, TILE_LON), ((0, 0), (0, 1), (0, 0)))

    order = jnp.arange(slot_count, dtype=jnp.int32)
    listed = (tile_src[:, :, 0] * LANES_T + tile_local).reshape(devices, slot_count)
    here = lax.dynamic_slice_in_dim(listed, outer * INNER, INNER, 0)
    src, loc = here // LANES_T, here % LANES_T
    target = src % INNER
    band_layer = src // INNER
    beside = jnp.where(outer == 0, 1, jnp.where(outer == outer_n - 1, outer_n - 2, -1))
    grouped = band_layer == beside
    target = jnp.where(grouped, INNER + target, target)
    same = (target[:, :, None] == target[:, None, :]) & (order[None, :] < order[:, None])[None]
    rank = jnp.sum(same.astype(jnp.int32), axis=2)
    places = jnp.arange(slots, dtype=jnp.int32)
    my_target = lax.dynamic_index_in_dim(target, inner, 0, keepdims=False)
    my_rank = lax.dynamic_index_in_dim(rank, inner, 0, keepdims=False)
    place = jnp.where(my_target < INNER, my_target * slots + my_rank, -1)
    hot = place[None, :] == jnp.arange(INNER * slots, dtype=jnp.int32)[:, None]
    splits = GROUP_ROWS // cap
    group_rows = jnp.arange(INNER * GROUP_ROWS, dtype=jnp.int32)
    row_owner, row_split, row_slot = group_rows // GROUP_ROWS, group_rows % GROUP_ROWS // cap, group_rows % cap
    in_group = (my_target[None, :] == INNER + row_owner[:, None]) & (my_rank[None, :] == row_slot[:, None])
    hot2 = in_group[:, None, :] & (row_split[:, None] == jnp.arange(splits, dtype=jnp.int32)[None, :])[:, :, None]
    hot2 = hot2.reshape(INNER * GROUP_ROWS, splits * slot_count)
    from_layer = jnp.where(outer == 1, 0, outer_n - 1)
    there = lax.dynamic_slice_in_dim(listed, from_layer * INNER, INNER, 0)
    src_end, loc_end = there // LANES_T, there % LANES_T
    to_me = src_end == me
    rank_end = jnp.sum((to_me[:, None, :] & (order[None, :] < order[:, None])[None]).astype(jnp.int32), axis=2)
    taken = to_me[:, None, :] & (rank_end[:, None, :] == jnp.arange(cap, dtype=jnp.int32)[None, :, None])
    tile_end = jnp.sum(jnp.where(taken, loc_end[:, None, :] + 1, 0), axis=2) - 1
    tile_end = jnp.broadcast_to(tile_end[:, None, :], (INNER, splits, cap)).reshape(INNER * GROUP_ROWS)
    sel2 = (tile_end[None, :, None] == (jnp.arange(wide, dtype=jnp.int32) % LANES_T)[None, None, :]) & (
        row_split[None, :, None] == jnp.arange(splits, dtype=jnp.int32)[:, None, None]
    )
    chosen = (target[:, None, :] == inner) & (rank[:, None, :] == places[None, :, None])
    code = band_layer * LANES_T + loc + 1
    named = jnp.sum(jnp.where(chosen, code[:, None, :], 0), axis=2).reshape(INNER * slots) - 1
    columns = jnp.arange(outer_n * wide, dtype=jnp.int32)
    column_code = (columns // wide) * LANES_T + columns % LANES_T
    sel = (named[:, None] == column_code[None, :]).astype(jnp.float32)
    group = ((columns % wide) // LANES_T)[:, None] == jnp.arange(128, dtype=jnp.int32)[None, :]
    live = (jnp.arange(KT, dtype=jnp.int32)[None, :] < tile_count[:, None]).reshape(slot_count)
    mine = (order // KT)[None, :] == jnp.arange(stations, dtype=jnp.int32)[:, None]
    hits = (mine & live[None, :])[:, :, None] & (place[None, :, None] == jnp.arange(INNER * slots, dtype=jnp.int32)[None, None, :])
    weights = jnp.sum(hits.astype(jnp.float32), axis=1)
    weights2 = jnp.sum(((mine & live[None, :])[:, None, :] & in_group[None]).astype(jnp.float32), axis=2)

    ext = rows + 2 * ITERS
    vmem = pl.BlockSpec(memory_space=pltpu.VMEM)
    dma = pltpu.SemaphoreType.DMA
    observed = pl.pallas_call(
        functools.partial(kernel, outer_n, slots, splits),
        out_shape=jax.ShapeDtypeStruct((stations, 128), jnp.float32),
        in_specs=[pl.BlockSpec(memory_space=pltpu.SMEM)] + [vmem] * 10,
        out_specs=vmem,
        scratch_shapes=[
            pltpu.VMEM((INNER * slots, footprint.shape[2]), jnp.bfloat16),
            pltpu.VMEM((INNER * slots, footprint.shape[2]), jnp.bfloat16),
            pltpu.VMEM((INNER * GROUP_ROWS, footprint.shape[2] // splits), jnp.bfloat16),
            pltpu.VMEM((INNER * GROUP_ROWS, footprint.shape[2] // splits), jnp.bfloat16),
            pltpu.VMEM((2, ITERS, wide, TILE_LON), jnp.bfloat16),
            pltpu.VMEM((2, ITERS, LANES_T, TILE_LON), jnp.float32),
            pltpu.VMEM((ext, wide, TILE_LON), jnp.float32),
            pltpu.VMEM((ext, wide, TILE_LON), jnp.float32),
            pltpu.VMEM((ext, LANES_T, TILE_LON), jnp.float32),
            pltpu.VMEM((rows, outer_n * wide, TILE_LON), jnp.bfloat16),
            pltpu.VMEM((INNER * slots, outer_n * wide), jnp.float32),
            pltpu.VMEM((INNER * slots, 128), jnp.float32),
            pltpu.VMEM((INNER * slots, 128), jnp.float32),
            pltpu.VMEM((INNER * GROUP_ROWS, 128), jnp.float32),
            pltpu.VMEM((INNER * GROUP_ROWS, 128), jnp.float32),
            dma((INNER, PIECES)), dma((INNER, PIECES)),
            dma((INNER,)), dma((INNER,)),
            dma((2, 2)), dma((2, 2)),
            dma((outer_n - 1, PIECES)), dma((outer_n - 1, PIECES)),
            dma((outer_n - 1, PIECES)), dma((outer_n - 1, PIECES)),
            dma((INNER,)), dma((INNER,)),
            dma((INNER,)), dma((INNER,)),
        ],
        compiler_params=pltpu.CompilerParams(
            collective_id=0, has_side_effects=True, vmem_limit_bytes=50 * 1024 * 1024
        ),
    )(
        diff_steps, footprint, hot.astype(jnp.bfloat16),
        hot2.astype(jnp.bfloat16), flux_t, coef_t, sel, sel2.astype(jnp.float32), group.astype(jnp.float32),
        weights, weights2,
    )
    return lax.all_gather(observed[:, :samples], "sample", axis=1, tiled=True)


def solution(mesh):
    in_specs = (
        P("sample", "station", None),
        P("station", None),
        P("sample"),
        P("station", None, None),
        P(),
        P(),
        P("station"),
    )
    out_specs = P("station", None)
    return jax.shard_map(body, mesh=mesh, in_specs=in_specs, out_specs=out_specs, check_vma=False)
```

```python
import functools

import jax
import jax.numpy as jnp
from jax import lax
from jax.experimental import pallas as pl
from jax.experimental.pallas import tpu as pltpu
from jax.sharding import PartitionSpec as P

TILE_LON = 512
TILES_DEV = 7
LANES_T = 8
KT = 4
ITERS = 6
INNER = 8
PIECES = 8
GROUP_ROWS = 16
MESH = pl.DeviceIdType.MESH


def east_west(x, lane, tile):
    width = x.shape[1]
    west = pltpu.roll(x, 1, 1)
    first = west[:, :128]
    before = jnp.where(tile == 0, pltpu.roll(first, 2, 0), pltpu.roll(first, 1, 0))
    first = jnp.where(lane == 0, before, first)
    west = jnp.concatenate([first, west[:, 128:]], axis=1)
    east = pltpu.roll(x, width - 1, 1)
    last = east[:, width - 128 :]
    after = jnp.where(tile == TILES_DEV - 1, pltpu.roll(last, 6, 0), pltpu.roll(last, 7, 0))
    last = jnp.where(lane == 127, after, last)
    east = jnp.concatenate([east[:, : width - 128], last], axis=1)
    return west, east


def kernel(
    outer_n, slots, splits,
    steps, prints, hot, hot2, flux, coef, sel, sel2, group, weights, weights2,
    out,
    send, arr, send2, arr2, halo_f, halo_c, field_a, field_b, cof, tiles, acc, val, ret, val2, ret2,
    f_send, f_recv, g_send, g_recv, h_send, h_recv, r_send, r_recv, l_send, l_recv, v_send, v_recv, w_send, w_recv,
):
    rows = flux.shape[0]
    wide = flux.shape[1]
    samples = wide // LANES_T
    count = outer_n * INNER
    me = lax.axis_index("station")
    outer, inner = me // INNER, lax.rem(me, INNER)
    base = outer * INNER
    has_up, has_down = me > 0, me < count - 1
    has_left, has_right = outer > 0, outer < outer_n - 1
    first, last = outer == 0, outer == outer_n - 1
    is_end = jnp.logical_or(first, last)
    is_next = jnp.logical_or(outer == 1, outer == outer_n - 2)
    other_base = jnp.where(first, 1, jnp.where(last, outer_n - 2, jnp.where(outer == 1, 0, outer_n - 1))) * INNER
    lone_left = jnp.logical_and(outer >= 2, outer <= outer_n - 2)
    lone_right = jnp.logical_and(outer >= 1, outer <= outer_n - 3)
    lone_up = jnp.logical_and(lone_left, inner == 0)
    lone_down = jnp.logical_and(lone_right, inner == INNER - 1)

    def peer(offset):
        return base + lax.rem(inner + offset, INNER)

    def across(offset):
        return other_base + lax.rem(inner + offset, INNER)

    barrier = pltpu.get_barrier_semaphore()

    def greet(device):
        pl.semaphore_signal(barrier, inc=1, device_id={"station": device}, device_id_type=MESH)

    for offset in range(1, INNER):
        greet(peer(offset))
    others = ((lone_left, -INNER), (lone_right, INNER), (lone_up, -1), (lone_down, 1))
    for there, step in others:
        @pl.when(there)
        def _():
            greet(me + step)

    paired = jnp.logical_or(is_end, is_next)

    @pl.when(paired)
    def _():
        for offset in range(INNER):
            greet(across(offset))
    pl.semaphore_wait(
        barrier,
        INNER - 1 + sum(jnp.where(there, 1, 0) for there, _ in others) + jnp.where(paired, INNER, 0),
    )

    def remote(src, dst, ssem, rsem, device):
        return pltpu.make_async_remote_copy(
            src_ref=src, dst_ref=dst, send_sem=ssem, recv_sem=rsem,
            device_id={"station": device}, device_id_type=MESH,
        )

    def halo_copies(way):
        step = -1 if way == 0 else 1
        cut = pl.ds(0, ITERS) if way == 0 else pl.ds(rows - ITERS, ITERS)
        return (
            remote(flux.at[cut], halo_f.at[1 - way], h_send.at[way, 0], h_recv.at[1 - way, 0], me + step),
            remote(coef.at[cut], halo_c.at[1 - way], h_send.at[way, 1], h_recv.at[1 - way, 1], me + step),
        )

    for way, there in ((0, has_up), (1, has_down)):
        @pl.when(there)
        def _():
            for copy in halo_copies(way):
                copy.start()

        @pl.when(jnp.logical_not(there))
        def _():
            halo_f[way] = jnp.zeros(halo_f.shape[1:], halo_f.dtype)
            halo_c[way] = jnp.zeros(halo_c.shape[1:], halo_c.dtype)

    cells = prints.shape[2]
    short = cells // splits

    def some_prints(at):
        block = prints[:, :, pl.ds(pl.multiple_of(at, 256), 256)]
        return block.reshape(block.shape[0] * KT, 256)

    own2 = pl.ds(pl.multiple_of(inner * GROUP_ROWS, GROUP_ROWS), GROUP_ROWS)

    def rows2(offset):
        return pl.ds(pl.multiple_of(lax.rem(inner + offset, INNER) * GROUP_ROWS, GROUP_ROWS), GROUP_ROWS)

    def group_copy(offset):
        return remote(send2.at[rows2(offset)], arr2.at[own2], g_send.at[offset], g_recv.at[offset], across(offset))

    @pl.when(is_end)
    def _():
        def pack2(i, carry):
            for j in range(2):
                at = i * 512 + j * 256
                stack = [some_prints(q * short + at) for q in range(splits)]
                packed = jnp.dot(hot2[...], jnp.concatenate(stack, axis=0), preferred_element_type=jnp.float32)
                send2[:, pl.ds(pl.multiple_of(at, 256), 256)] = packed.astype(jnp.bfloat16)
            return carry

        lax.fori_loop(0, short // 512, pack2, 0)
        for offset in range(INNER):
            group_copy(offset).start()
        missing = jnp.where(first, 1, outer_n - 2)

        def clear(r, carry):
            tiles[r, pl.ds(pl.multiple_of(missing * wide, wide), wide), :] = jnp.zeros((wide, TILE_LON), jnp.bfloat16)
            return carry

        lax.fori_loop(0, rows, clear, 0)

    length = cells // PIECES

    def print_copy(offset, c):
        target = peer(offset)
        lanes = pl.ds(pl.multiple_of(c * length, length), length)
        to_rows = pl.ds(pl.multiple_of(lax.rem(inner + offset, INNER) * slots, slots), slots)
        my_rows = pl.ds(pl.multiple_of(inner * slots, slots), slots)
        return remote(send.at[to_rows, lanes], arr.at[my_rows, lanes], f_send.at[offset, c], f_recv.at[offset, c], target)

    own = pl.ds(pl.multiple_of(inner * slots, slots), slots)

    def send_prints(c):
        for j in range(length // 256):
            at = c * length + j * 256
            packed = jnp.dot(hot[...], some_prints(at), preferred_element_type=jnp.float32)
            send[:, pl.ds(pl.multiple_of(at, 256), 256)] = packed.astype(jnp.bfloat16)
        for offset in range(1, INNER):
            print_copy(offset, c).start()

    def load(r, carry):
        field_a[r + ITERS] = flux[r].astype(jnp.float32)
        cof[r + ITERS] = coef[r]
        return carry

    lax.fori_loop(0, rows, load, 0)
    for way, there in ((0, has_up), (1, has_down)):
        @pl.when(there)
        def _():
            for copy in halo_copies(way):
                copy.wait_send()
            remote(flux.at[pl.ds(0, ITERS)], halo_f.at[way], h_send.at[way, 0], h_recv.at[way, 0], me).wait_recv()
            remote(coef.at[pl.ds(0, ITERS)], halo_c.at[way], h_send.at[way, 1], h_recv.at[way, 1], me).wait_recv()

    def load_halo(r, carry):
        field_a[r] = halo_f[0, r].astype(jnp.float32)
        cof[r] = halo_c[0, r]
        field_a[r + ITERS + rows] = halo_f[1, r].astype(jnp.float32)
        cof[r + ITERS + rows] = halo_c[1, r]
        return carry

    lax.fori_loop(0, ITERS, load_halo, 0)

    lane = lax.broadcasted_iota(jnp.int32, (LANES_T, 128), 1)
    tile = lax.broadcasted_iota(jnp.int32, (LANES_T, 128), 0)

    def updated(src, r, k, s):
        cut = slice(s * LANES_T, (s + 1) * LANES_T)
        center = src[r, cut, :]
        west, east = east_west(center, lane, tile)
        lap = src[r - 1, cut, :] + src[r + 1, cut, :] + west + east - 4.0 * center
        return center + jnp.where(k < steps[s], 1.0, 0.0) * cof[r] * lap

    piece = rows // PIECES

    def block_copy(block, c, k, to_right):
        at = tiles.at[pl.ds(c * piece, piece), pl.ds(pl.multiple_of(block * wide, wide), wide), :]
        if to_right:
            return remote(at, at, r_send.at[k, c], r_recv.at[k, c], me + INNER)
        return remote(at, at, l_send.at[k, c], l_recv.at[k, c], me - INNER)

    def goes(there, k, to_right):
        there = jnp.logical_and(there, has_right if to_right else has_left)
        if k == 0:
            there = jnp.logical_and(there, outer != (outer_n - 2 if to_right else 1))
        return there

    def start_block(block, c, k, to_right, there):
        @pl.when(goes(there, k, to_right))
        def _():
            block_copy(block, c, k, to_right).start()

    mine = pl.ds(pl.multiple_of(outer * wide, wide), wide)

    def step_row(r, k):
        src, dst = (field_a, field_b) if k % 2 == 0 else (field_b, field_a)
        done = [updated(src, r, k, s) for s in range(samples)]
        if k == ITERS - 1:
            tiles[r - ITERS, mine, :] = jnp.concatenate(done, axis=0).astype(jnp.bfloat16)
        else:
            for s in range(samples):
                dst[r, s * LANES_T : (s + 1) * LANES_T, :] = done[s]

    def send_piece(c):
        start_block(outer, c, 0, True, has_right)
        start_block(outer, c, 0, False, has_left)

    for k in range(ITERS):
        def row_pair(i, carry, k=k):
            step_row(k + 1 + 2 * i, k)
            step_row(k + 2 + 2 * i, k)
            return carry

        lax.fori_loop(0, piece // 2 + ITERS - 1 - k, row_pair, 0)
    send_piece(0)
    send_prints(0)

    def reach(k):
        from_left, from_right = outer - 1 - k >= 0, outer + 1 + k < outer_n
        if k == 0:
            from_left = jnp.logical_and(from_left, jnp.logical_not(last))
            from_right = jnp.logical_and(from_right, jnp.logical_not(first))
        return from_left, from_right

    def relay(c, k, begun=True):
        from_left, from_right = (jnp.logical_and(there, begun) for there in reach(k))

        @pl.when(from_left)
        def _():
            block_copy(outer - 1 - k, c, k, True).wait_recv()

        if k < outer_n - 2:
            start_block(outer - 1 - k, c, k + 1, True, from_left)

        @pl.when(from_right)
        def _():
            block_copy(outer + 1 + k, c, k, False).wait_recv()

        if k < outer_n - 2:
            start_block(outer + 1 + k, c, k + 1, False, from_right)

    def next_piece(c, carry):
        for k in range(ITERS):
            for j in range(piece):
                step_row(c * piece + 2 * ITERS - 1 - k + j, k)
        send_piece(c)
        relay(c - 2, 0, c >= 2)
        relay(c - 4, 1, c >= 4)
        send_prints(c)
        return carry

    lax.fori_loop(1, PIECES, next_piece, 0)
    for c in range(PIECES - 2, PIECES):
        relay(c, 0)
    for c in range(PIECES - 4, PIECES):
        relay(c, 1)
    arr[own, :] = send[own, :]

    def multiply(c):
        for offset in range(1, INNER):
            print_copy(offset, c).wait_recv()
        total = jnp.zeros(acc.shape, jnp.float32) if c == 0 else acc[...]
        for r in range(c * piece, (c + 1) * piece):
            total = total + lax.dot_general(
                arr[:, r * TILE_LON : (r + 1) * TILE_LON], tiles[r], (((1,), (1,)), ((), ())),
                preferred_element_type=jnp.float32,
            )
        acc[...] = total

    def value_copy2(offset):
        return remote(val2.at[rows2(offset)], ret2.at[own2], w_send.at[offset], w_recv.at[offset], across(offset))

    def group_values():
        for offset in range(INNER):
            group_copy(offset).wait_recv()
        per_split = rows // splits
        total = jnp.zeros(sel2.shape[1:], jnp.float32)
        for q in range(splits):
            def add_row(r, part, q=q):
                return part + lax.dot_general(
                    arr2[:, pl.ds(pl.multiple_of(r * TILE_LON, TILE_LON), TILE_LON)],
                    tiles[q * per_split + r, mine, :], (((1,), (1,)), ((), ())),
                    preferred_element_type=jnp.float32,
                )

            part = jnp.zeros(sel2.shape[1:], jnp.float32)
            for r in range(per_split):
                part = add_row(r, part)
            total = total + part * sel2[q]
        val2[...] = jnp.dot(total, group[:wide, :], precision=lax.Precision.HIGHEST, preferred_element_type=jnp.float32)
        for offset in range(INNER):
            value_copy2(offset).start()

    pl.when(is_next)(group_values)
    for k in range(2, outer_n - 1):
        for c in range(PIECES):
            relay(c, k)
            if k == outer_n - 2:
                multiply(c)

    val[...] = jnp.dot(acc[...] * sel[...], group[...], precision=lax.Precision.HIGHEST, preferred_element_type=jnp.float32)

    def value_copy(offset):
        to_rows = pl.ds(pl.multiple_of(lax.rem(inner + offset, INNER) * slots, slots), slots)
        return remote(val.at[to_rows], ret.at[own], v_send.at[offset], v_recv.at[offset], peer(offset))

    for offset in range(1, INNER):
        value_copy(offset).start()
    ret[own, :] = val[own, :]
    for offset in range(1, INNER):
        value_copy(offset).wait_recv()
    out[...] = jnp.dot(weights[...], ret[...], precision=lax.Precision.HIGHEST, preferred_element_type=jnp.float32)

    @pl.when(is_end)
    def _():
        for offset in range(INNER):
            value_copy2(offset).wait_recv()
        out[...] += jnp.dot(weights2[...], ret2[...], precision=lax.Precision.HIGHEST, preferred_element_type=jnp.float32)
        for offset in range(INNER):
            group_copy(offset).wait_send()

    @pl.when(is_next)
    def _():
        for offset in range(INNER):
            value_copy2(offset).wait_send()

    for offset in range(1, INNER):
        value_copy(offset).wait_send()
        for c in range(PIECES):
            print_copy(offset, c).wait_send()
    for k in range(outer_n - 1):
        for c in range(PIECES):
            @pl.when(goes(outer - k >= 0, k, True))
            def _():
                block_copy(outer - k, c, k, True).wait_send()

            @pl.when(goes(outer + k < outer_n, k, False))
            def _():
                block_copy(outer + k, c, k, False).wait_send()


def body(flux, coeff, diff_steps, footprint, tile_src, tile_local, tile_count):
    samples, rows, _ = flux.shape
    stations = footprint.shape[0]
    devices = lax.axis_size("station")
    outer_n = devices // INNER
    me = lax.axis_index("station")
    outer, inner = me // INNER, me % INNER
    slot_count = stations * KT
    cap = 2 * max(1, (slot_count + devices - 1) // devices)
    slots = outer_n * cap
    wide = samples * LANES_T

    flux_t = flux.reshape(samples, rows, TILES_DEV, TILE_LON).transpose(1, 0, 2, 3)
    flux_t = jnp.pad(flux_t, ((0, 0), (0, 0), (0, 1), (0, 0))).reshape(rows, wide, TILE_LON)
    coef_t = jnp.pad(coeff.reshape(rows, TILES_DEV, TILE_LON), ((0, 0), (0, 1), (0, 0)))

    order = jnp.arange(slot_count, dtype=jnp.int32)
    listed = (tile_src[:, :, 0] * LANES_T + tile_local).reshape(devices, slot_count)
    here = lax.dynamic_slice_in_dim(listed, outer * INNER, INNER, 0)
    src, loc = here // LANES_T, here % LANES_T
    target = src % INNER
    band_layer = src // INNER
    beside = jnp.where(outer == 0, 1, jnp.where(outer == outer_n - 1, outer_n - 2, -1))
    grouped = band_layer == beside
    target = jnp.where(grouped, INNER + target, target)
    same = (target[:, :, None] == target[:, None, :]) & (order[None, :] < order[:, None])[None]
    rank = jnp.sum(same.astype(jnp.int32), axis=2)
    places = jnp.arange(slots, dtype=jnp.int32)
    my_target = lax.dynamic_index_in_dim(target, inner, 0, keepdims=False)
    my_rank = lax.dynamic_index_in_dim(rank, inner, 0, keepdims=False)
    place = jnp.where(my_target < INNER, my_target * slots + my_rank, -1)
    hot = place[None, :] == jnp.arange(INNER * slots, dtype=jnp.int32)[:, None]
    splits = GROUP_ROWS // cap
    group_rows = jnp.arange(INNER * GROUP_ROWS, dtype=jnp.int32)
    row_owner, row_split, row_slot = group_rows // GROUP_ROWS, group_rows % GROUP_ROWS // cap, group_rows % cap
    in_group = (my_target[None, :] == INNER + row_owner[:, None]) & (my_rank[None, :] == row_slot[:, None])
    hot2 = in_group[:, None, :] & (row_split[:, None] == jnp.arange(splits, dtype=jnp.int32)[None, :])[:, :, None]
    hot2 = hot2.reshape(INNER * GROUP_ROWS, splits * slot_count)
    from_layer = jnp.where(outer == 1, 0, outer_n - 1)
    there = lax.dynamic_slice_in_dim(listed, from_layer * INNER, INNER, 0)
    src_end, loc_end = there // LANES_T, there % LANES_T
    to_me = src_end == me
    rank_end = jnp.sum((to_me[:, None, :] & (order[None, :] < order[:, None])[None]).astype(jnp.int32), axis=2)
    taken = to_me[:, None, :] & (rank_end[:, None, :] == jnp.arange(cap, dtype=jnp.int32)[None, :, None])
    tile_end = jnp.sum(jnp.where(taken, loc_end[:, None, :] + 1, 0), axis=2) - 1
    tile_end = jnp.broadcast_to(tile_end[:, None, :], (INNER, splits, cap)).reshape(INNER * GROUP_ROWS)
    sel2 = (tile_end[None, :, None] == (jnp.arange(wide, dtype=jnp.int32) % LANES_T)[None, None, :]) & (
        row_split[None, :, None] == jnp.arange(splits, dtype=jnp.int32)[:, None, None]
    )
    chosen = (target[:, None, :] == inner) & (rank[:, None, :] == places[None, :, None])
    code = band_layer * LANES_T + loc + 1
    named = jnp.sum(jnp.where(chosen, code[:, None, :], 0), axis=2).reshape(INNER * slots) - 1
    columns = jnp.arange(outer_n * wide, dtype=jnp.int32)
    column_code = (columns // wide) * LANES_T + columns % LANES_T
    sel = (named[:, None] == column_code[None, :]).astype(jnp.float32)
    group = ((columns % wide) // LANES_T)[:, None] == jnp.arange(128, dtype=jnp.int32)[None, :]
    live = (jnp.arange(KT, dtype=jnp.int32)[None, :] < tile_count[:, None]).reshape(slot_count)
    mine = (order // KT)[None, :] == jnp.arange(stations, dtype=jnp.int32)[:, None]
    hits = (mine & live[None, :])[:, :, None] & (place[None, :, None] == jnp.arange(INNER * slots, dtype=jnp.int32)[None, None, :])
    weights = jnp.sum(hits.astype(jnp.float32), axis=1)
    weights2 = jnp.sum(((mine & live[None, :])[:, None, :] & in_group[None]).astype(jnp.float32), axis=2)

    ext = rows + 2 * ITERS
    vmem = pl.BlockSpec(memory_space=pltpu.VMEM)
    dma = pltpu.SemaphoreType.DMA
    observed = pl.pallas_call(
        functools.partial(kernel, outer_n, slots, splits),
        out_shape=jax.ShapeDtypeStruct((stations, 128), jnp.float32),
        in_specs=[pl.BlockSpec(memory_space=pltpu.SMEM)] + [vmem] * 10,
        out_specs=vmem,
        scratch_shapes=[
            pltpu.VMEM((INNER * slots, footprint.shape[2]), jnp.bfloat16),
            pltpu.VMEM((INNER * slots, footprint.shape[2]), jnp.bfloat16),
            pltpu.VMEM((INNER * GROUP_ROWS, footprint.shape[2] // splits), jnp.bfloat16),
            pltpu.VMEM((INNER * GROUP_ROWS, footprint.shape[2] // splits), jnp.bfloat16),
            pltpu.VMEM((2, ITERS, wide, TILE_LON), jnp.bfloat16),
            pltpu.VMEM((2, ITERS, LANES_T, TILE_LON), jnp.float32),
            pltpu.VMEM((ext, wide, TILE_LON), jnp.float32),
            pltpu.VMEM((ext, wide, TILE_LON), jnp.float32),
            pltpu.VMEM((ext, LANES_T, TILE_LON), jnp.float32),
            pltpu.VMEM((rows, outer_n * wide, TILE_LON), jnp.bfloat16),
            pltpu.VMEM((INNER * slots, outer_n * wide), jnp.float32),
            pltpu.VMEM((INNER * slots, 128), jnp.float32),
            pltpu.VMEM((INNER * slots, 128), jnp.float32),
            pltpu.VMEM((INNER * GROUP_ROWS, 128), jnp.float32),
            pltpu.VMEM((INNER * GROUP_ROWS, 128), jnp.float32),
            dma((INNER, PIECES)), dma((INNER, PIECES)),
            dma((INNER,)), dma((INNER,)),
            dma((2, 2)), dma((2, 2)),
            dma((outer_n - 1, PIECES)), dma((outer_n - 1, PIECES)),
            dma((outer_n - 1, PIECES)), dma((outer_n - 1, PIECES)),
            dma((INNER,)), dma((INNER,)),
            dma((INNER,)), dma((INNER,)),
        ],
        compiler_params=pltpu.CompilerParams(
            collective_id=0, has_side_effects=True, vmem_limit_bytes=50 * 1024 * 1024
        ),
    )(
        diff_steps, footprint, hot.astype(jnp.bfloat16),
        hot2.astype(jnp.bfloat16), flux_t, coef_t, sel, sel2.astype(jnp.float32), group.astype(jnp.float32),
        weights, weights2,
    )
    return lax.all_gather(observed[:, :samples], "sample", axis=1, tiled=True)


def solution(mesh):
    in_specs = (
        P("sample", "station", None),
        P("station", None),
        P("sample"),
        P("station", None, None),
        P(),
        P(),
        P("station"),
    )
    out_specs = P("station", None)
    return jax.shard_map(body, mesh=mesh, in_specs=in_specs, out_specs=out_specs, check_vma=False)
```
